256 devices in a mesh: row: 32 (over x, z_hi, core), col: 8 (over y, z_lo).
Axes of the slice: x: 4, y: 4, z: 8 (z_hi: 4, z_lo: 2; z = z_hi * 2 + z_lo), core: 2. Of those that a mesh axis runs over, the one named last changes fastest.
Arguments:
- x_train: bfloat16 [64, 32768], P(None, 'col'), may hold values from -8 to 8
- targets: float32 [32768], P('col'), may hold values from -6 to 6
- noise_draws: float32 [32768, 256], P('col', 'row'), may hold values from -3 to 3
- alpha_init: float32 [32768, 256], P('col', 'row'), may hold values from -6 to 6
- velocity_init: float32 [32768, 256], P('col', 'row'), may hold values from -3 to 3
- frequencies: bfloat16 [64, 4096], P(None, 'col'), may hold values from -5 to 5
- phases: float32 [4096], P('col'), may hold values from -3.140625 to 3.140625
- path_weights: bfloat16 [4096, 256], P('col'), may hold values from -6 to 6
- x_window: bfloat16 [64, 65536], P(None, 'row'), may hold values from -6 to 6
- batch_index: int32 [3, 16384], replicated, may hold values from 0 to 32767, as said below
Outputs:
- alpha_out: float32 [32768, 256], P('col', 'row')
- velocity_out: float32 [32768, 256], P('col', 'row')
- prior_window: float32 [256, 65536], P('col', 'row')
The draws below stay inside these ranges and needn't reach their ends.
Inputs may be any that keep to these rules, and one draw needn't show every extreme that they name: `batch_index`: row b of every step names a training point of group g = (b // 64) % 8, that is a number from g * 4096 to (g + 1) * 4096 - 1; points may repeat.
All inputs are finite; a program needn't handle non-finite values.
Results may differ from the reference program's by a relative error of at most 0.0039.
Values may be sent and summed in bfloat16 or wider, within the bound.
No kernel may reach another device: no remote copies, remote signals or barrier semaphores. Data moves between devices by JAX's collectives and lax.ppermute only.
A program may use at most 64 MiB of HBM per device.

```python
import jax
import jax.numpy as jnp
from jax import lax

D_IN = 64
FEAT = 4096
PATHS = 256
STEPS = 3
TRAIN_DEV = 4096
BATCH_DEV = 512
WINDOW_DEV = 2048
TRAIN = 32768
BATCH = 16384
WINDOW = 65536
N_ROW = 32


def draw_x_train(key, part):
    clusters = max(TRAIN // 4, 1)
    center_scale = (40.0 / D_IN) ** 0.5
    offset_scale = (1.0 / D_IN) ** 0.5
    member = jax.random.randint(jax.random.fold_in(key, 14), (TRAIN,), 0, clusters)
    center_key = jax.random.fold_in(key, 15)
    offset_key = jax.random.fold_in(key, 16)
    centers = center_scale * jax.random.normal(center_key, (D_IN, clusters), jnp.float32)
    offsets = offset_scale * jax.random.normal(offset_key, (D_IN, TRAIN), jnp.float32)
    points = jnp.take(centers, member, axis=1) + offsets
    return jnp.clip(points, -8.0, 8.0).astype(jnp.bfloat16)


def draw_batch_index(key, part):
    col_groups = TRAIN // TRAIN_DEV
    own_rows = BATCH_DEV // col_groups
    positions = jnp.arange(BATCH)
    group_ids = positions // own_rows % col_groups
    offsets = jax.random.randint(jax.random.fold_in(key, 21), (STEPS, BATCH), 0, TRAIN_DEV)
    return (group_ids[None, :] * TRAIN_DEV + offsets).astype(jnp.int32)


def level_of(key, shape, cuts, smallest, top_value):
    loudness = 1.0
    for position, shards_of in cuts:
        steps = jax.random.uniform(jax.random.fold_in(jax.random.fold_in(key, 6), position), (shards_of,), jnp.float32, smallest / len(cuts), top_value / len(cuts))
        loudness = loudness * jnp.repeat(jnp.exp(steps), shape[position] // shards_of).reshape((-1,) + (1,) * (len(shape) - 1 - position))
    return loudness


def gaussian(rng, extent, deviation, most, pieces=(), kind=jnp.bfloat16):
    entries = deviation * jax.random.normal(rng, extent, jnp.float32)
    if pieces:
        entries = entries * level_of(rng, extent, pieces, -0.22, 0.18)
    return jnp.clip(entries, -most, most).astype(kind)


def setup_inputs(seed: int = 0) -> dict:
    key_list = jax.random.split(jax.random.key(seed), 11)
    x_train = draw_x_train(jax.random.fold_in(key_list[10], 71), 0)
    targets = gaussian(key_list[1], (TRAIN,), 1.0, 6.0, ((0, 8),), jnp.float32)
    noise_draws = gaussian(key_list[2], (TRAIN, PATHS), 0.5, 3.0, ((0, 8), (1, 32)), jnp.float32)
    alpha_init = gaussian(key_list[3], (TRAIN, PATHS), 1.0, 6.0, ((0, 8), (1, 32)), jnp.float32)
    velocity_init = gaussian(key_list[4], (TRAIN, PATHS), 0.5, 3.0, ((0, 8), (1, 32)), jnp.float32)
    frequencies = gaussian(key_list[5], (D_IN, FEAT), 0.87, 5.0, ((1, 8),))
    phases = jnp.clip(jax.random.uniform(key_list[6], (FEAT,), jnp.float32, -3.140625, 3.140625), -3.140625, 3.140625)
    path_weights = gaussian(key_list[7], (FEAT, PATHS), 1.0, 6.0, ((0, 8),))
    x_window = gaussian(key_list[8], (D_IN, WINDOW), 1.0, 6.0, ((1, 32),))
    batch_index = draw_batch_index(jax.random.fold_in(key_list[10], 71), 0)
    return dict(x_train=x_train, targets=targets, noise_draws=noise_draws, alpha_init=alpha_init, velocity_init=velocity_init, frequencies=frequencies, phases=phases, path_weights=path_weights, x_window=x_window, batch_index=batch_index)


SQRT_THREE = 1.7320508075688772
LENGTH = 1.15
NOISE_VAR = 0.25
MOMENTUM = 0.9
STEP_SIZE = 0.5
HIGH = lax.Precision.HIGHEST

def features(points, frequencies, phases):
    phase_arg = jnp.dot(frequencies.astype(jnp.float32).T, points.astype(jnp.float32), precision=HIGH)
    factor = (2.0 / FEAT) ** 0.5
    return (factor * jnp.cos(phase_arg + phases[:, None])).astype(jnp.bfloat16)

def kernel_rows(points, x_train, train_norm):
    inner_prod = jnp.dot(points.astype(jnp.float32).T, x_train.astype(jnp.float32), precision=HIGH)
    point_norm = lax.optimization_barrier(jnp.sum(jnp.square(points.astype(jnp.float32)), axis=0))
    dist_sq = jnp.maximum(point_norm[:, None] + train_norm[None, :] - 2.0 * inner_prod, 0.0)
    scaled = SQRT_THREE / LENGTH * jnp.sqrt(dist_sq)
    return ((1.0 + scaled) * jnp.exp(-scaled)).astype(jnp.bfloat16)

def reference(x_train, targets, noise_draws, alpha_init, velocity_init, frequencies, phases, path_weights, x_window, batch_index):
    weights_wide = path_weights.astype(jnp.float32)
    window_blocks = x_window.reshape(D_IN, N_ROW, WINDOW_DEV).transpose(1, 0, 2)

    def window_block(points):
        phi_block = lax.optimization_barrier(features(points, frequencies, phases)).astype(jnp.float32)
        return jnp.dot(weights_wide.T, phi_block, precision=HIGH)
    prior_blocks = lax.map(window_block, window_blocks)
    prior_window = prior_blocks.transpose(1, 0, 2).reshape(PATHS, WINDOW)
    train_norm = lax.optimization_barrier(jnp.sum(jnp.square(x_train.astype(jnp.float32)), axis=0))
    block_rows = min(256, BATCH)
    alpha = alpha_init
    velocity = velocity_init
    for step_id in range(STEPS):
        index_now = batch_index[step_id].astype(jnp.int32)
        points = jnp.take(x_train, index_now, axis=1)
        coeffs = lax.optimization_barrier(alpha.astype(jnp.bfloat16)).astype(jnp.float32)
        point_blocks = points.reshape(D_IN, BATCH // block_rows, block_rows).transpose(1, 0, 2)

        def batch_block(block_points):
            kernel = lax.optimization_barrier(kernel_rows(block_points, x_train, train_norm)).astype(jnp.float32)
            coupled = jnp.dot(kernel, coeffs, precision=HIGH)
            phi_block = lax.optimization_barrier(features(block_points, frequencies, phases)).astype(jnp.float32)
            return coupled + jnp.dot(phi_block.T, weights_wide, precision=HIGH)
        batch_sum = lax.map(batch_block, point_blocks).reshape(BATCH, PATHS)
        row_terms = batch_sum + NOISE_VAR * alpha[index_now] - targets[index_now][:, None] + noise_draws[index_now]
        gradient = jnp.zeros_like(alpha).at[index_now].add(row_terms)
        velocity = MOMENTUM * velocity - STEP_SIZE * gradient
        alpha = alpha + velocity
    return (alpha, velocity, prior_window)
```

```python
import jax
import jax.numpy as jnp
import numpy as np
from jax import lax
from jax.experimental import pallas as pl
from jax.experimental.pallas import tpu as pltpu
from jax.sharding import PartitionSpec as P

STEPS = 3
NOISE_VAR = 0.25
MOMENTUM = 0.9
STEP_SIZE = 0.5
LENGTH = 1.15
F32 = jnp.float32
BF16 = jnp.bfloat16
PI = float(np.pi)
PI_HIGH = 3.140625
PI_LOW = PI - PI_HIGH
LN2 = float(np.log(2.0))
KAPPA = float(3.0 / LENGTH**2 / np.log(2.0) ** 2)
NN = (((1,), (0,)), ((), ()))
NT = (((1,), (1,)), ((), ()))


def cosine_fit():
    top = (np.pi / 2 + 1e-4) ** 2
    nodes = (np.cos((2 * np.arange(200) + 1) * np.pi / 400) + 1) * top / 2
    fit = np.polynomial.chebyshev.Chebyshev.fit(nodes, np.cos(np.sqrt(nodes)), 5, domain=[0, top])
    return [float(v) for v in fit.convert(kind=np.polynomial.Polynomial).coef]


COS_COEFS = cosine_fit()


def dot(a, b, dims=NN):
    return lax.dot_general(a, b, dims, preferred_element_type=F32)


def scaled_cos(half_arg, factor):
    turns = jnp.round(half_arg * (1.0 / PI))
    h = (half_arg - turns * PI_HIGH) - turns * PI_LOW
    z = h * h
    c = jnp.full_like(z, COS_COEFS[-1])
    for coef in COS_COEFS[-2::-1]:
        c = c * z + coef
    return c * c * (2.0 * factor) - factor


def matern_kernel(p_ref, b_ref, o_ref, *, chunk):
    b = b_ref[...]
    wide = b.astype(F32)
    b_norm = jnp.sum(wide * wide, axis=0, keepdims=True)
    for i in range(0, p_ref.shape[0], chunk):
        p = p_ref[i : i + chunk, :].astype(F32)
        p_norm = jnp.sum(p * p, axis=1, keepdims=True)
        inner = dot((p * -2.0).astype(BF16), b)
        dist = jnp.maximum((inner + p_norm + b_norm) * KAPPA, 1e-30)
        u = dist * lax.rsqrt(dist)
        value = (u * LN2 + 1.0) * jnp.exp2(-u)
        o_ref[i : i + chunk, :] = value.astype(BF16)


def matern(points, others, block=512, chunk=128):
    rows, cols = points.shape[0], others.shape[1]
    return pl.pallas_call(
        lambda *refs: matern_kernel(*refs, chunk=chunk),
        grid=(cols // block,),
        in_specs=[
            pl.BlockSpec((rows, points.shape[1]), lambda i: (0, 0)),
            pl.BlockSpec((others.shape[0], block), lambda i: (0, i)),
        ],
        out_specs=pl.BlockSpec((rows, block), lambda i: (0, i)),
        out_shape=jax.ShapeDtypeStruct((rows, cols), BF16),
        compiler_params=pltpu.CompilerParams(vmem_limit_bytes=24 << 20),
        cost_estimate=pl.CostEstimate(
            flops=12 * rows * cols, bytes_accessed=2 * rows * cols, transcendentals=2 * rows * cols
        ),
        name="matern",
    )(points, others)


def matern_same_kernel(p_ref, b_ref, pid_ref, bid_ref, o_ref, *, chunk):
    b = b_ref[...]
    wide = b.astype(F32)
    b_norm = jnp.sum(wide * wide, axis=0, keepdims=True)
    bid = bid_ref[...]
    for i in range(0, p_ref.shape[0], chunk):
        p = p_ref[i : i + chunk, :].astype(F32)
        p_norm = jnp.sum(p * p, axis=1, keepdims=True)
        inner = dot((p * -2.0).astype(BF16), b)
        dist = jnp.maximum((inner + p_norm + b_norm) * KAPPA, 1e-30)
        u = dist * lax.rsqrt(dist)
        value = (u * LN2 + 1.0) * jnp.exp2(-u)
        same = pid_ref[i : i + chunk, :] == bid
        o_ref[i : i + chunk, :] = (value + jnp.where(same, NOISE_VAR, 0.0)).astype(BF16)


def matern_same(points, others, point_ids, other_ids, block=512, chunk=128):
    rows, cols = points.shape[0], others.shape[1]
    return pl.pallas_call(
        lambda *refs: matern_same_kernel(*refs, chunk=chunk),
        grid=(cols // block,),
        in_specs=[
            pl.BlockSpec((rows, points.shape[1]), lambda i: (0, 0)),
            pl.BlockSpec((others.shape[0], block), lambda i: (0, i)),
            pl.BlockSpec((rows, 1), lambda i: (0, 0)),
            pl.BlockSpec((1, block), lambda i: (0, i)),
        ],
        out_specs=pl.BlockSpec((rows, block), lambda i: (0, i)),
        out_shape=jax.ShapeDtypeStruct((rows, cols), BF16),
        compiler_params=pltpu.CompilerParams(vmem_limit_bytes=24 << 20),
        cost_estimate=pl.CostEstimate(
            flops=14 * rows * cols, bytes_accessed=2 * rows * cols, transcendentals=2 * rows * cols
        ),
        name="matern_same",
    )(points, others, point_ids, other_ids)


def batch_prior_kernel(p_ref, f_ref, ph_ref, w_ref, o_ref, *, factor, chunk):
    freq = f_ref[...] * BF16(0.5)
    half_phase = ph_ref[...] * 0.5
    for i in range(0, p_ref.shape[0], chunk):
        arg = dot(p_ref[i : i + chunk, :], freq) + half_phase
        phi = scaled_cos(arg, factor).astype(BF16)
        o_ref[i : i + chunk, :] = dot(phi, w_ref[...])


def batch_prior(points, frequencies, phases, weights, factor, block=512, chunk=128):
    rows, feats, paths = points.shape[0], frequencies.shape[1], weights.shape[1]
    return pl.pallas_call(
        lambda *refs: batch_prior_kernel(*refs, factor=factor, chunk=chunk),
        grid=(rows // block,),
        in_specs=[
            pl.BlockSpec((block, points.shape[1]), lambda i: (i, 0)),
            pl.BlockSpec(frequencies.shape, lambda i: (0, 0)),
            pl.BlockSpec((1, feats), lambda i: (0, 0)),
            pl.BlockSpec((feats, paths), lambda i: (0, 0)),
        ],
        out_specs=pl.BlockSpec((block, paths), lambda i: (i, 0)),
        out_shape=jax.ShapeDtypeStruct((rows, paths), F32),
        compiler_params=pltpu.CompilerParams(vmem_limit_bytes=24 << 20),
        cost_estimate=pl.CostEstimate(
            flops=24 * rows * feats, bytes_accessed=4 * rows * paths, transcendentals=rows * feats
        ),
        name="batch_prior",
    )(points, frequencies, phases[None, :], weights)


def window_kernel(f_ref, ph_ref, w_ref, x_ref, o_ref, *, factor, chunk):
    freq = f_ref[...] * BF16(0.5)
    half_phase = ph_ref[...] * 0.5
    total = None
    for i in range(0, f_ref.shape[0], chunk):
        arg = dot(freq[i : i + chunk, :], x_ref[...]) + half_phase[i : i + chunk, :]
        phi = scaled_cos(arg, factor).astype(BF16)
        part = dot(w_ref[:, i : i + chunk], phi)
        total = part if total is None else total + part
    o_ref[...] = total


def window_prior(frequencies, phases, weights, x_window, factor, block=256, chunk=128):
    feats, paths, window = frequencies.shape[1], weights.shape[1], x_window.shape[1]
    return pl.pallas_call(
        lambda *refs: window_kernel(*refs, factor=factor, chunk=chunk),
        grid=(window // block,),
        in_specs=[
            pl.BlockSpec((feats, frequencies.shape[0]), lambda i: (0, 0)),
            pl.BlockSpec((feats, 1), lambda i: (0, 0)),
            pl.BlockSpec((paths, feats), lambda i: (0, 0)),
            pl.BlockSpec((x_window.shape[0], block), lambda i: (0, i)),
        ],
        out_specs=pl.BlockSpec((paths, block), lambda i: (0, i)),
        out_shape=jax.ShapeDtypeStruct((paths, window), F32),
        compiler_params=pltpu.CompilerParams(vmem_limit_bytes=24 << 20),
        cost_estimate=pl.CostEstimate(
            flops=24 * feats * window, bytes_accessed=4 * paths * window, transcendentals=feats * window
        ),
        name="window_prior",
    )(frequencies.T, phases[:, None], weights.T, x_window)


def pick_rows_kernel(i_ref, x_ref, o_ref):
    index = i_ref[...]
    high, low = index & 255, index >> 8
    onehot = (lax.broadcasted_iota(jnp.int32, (index.shape[0], 256), 1) == high).astype(F32).astype(BF16)
    total = jnp.zeros(o_ref.shape, F32)
    for part in range(x_ref.shape[1] // 256):
        found = dot(onehot, x_ref[:, part * 256 : (part + 1) * 256], NT)
        total = total + jnp.where(low == part, found, 0.0)
    o_ref[...] = total.astype(BF16)


def pick_rows(index, x_train):
    return pl.pallas_call(
        pick_rows_kernel,
        out_shape=jax.ShapeDtypeStruct((index.shape[0], x_train.shape[0]), BF16),
        name="pick_rows",
    )(index[:, None], x_train)


def pick_cols_kernel(i_ref, x_ref, o_ref):
    index = i_ref[0]
    high, low = index & 255, index >> 8
    onehot = (lax.broadcasted_iota(jnp.int32, (256, index.shape[1]), 0) == high).astype(F32).astype(BF16)
    total = jnp.zeros(o_ref.shape[1:], F32)
    for part in range(x_ref.shape[1] // 256):
        found = dot(x_ref[:, part * 256 : (part + 1) * 256], onehot)
        total = total + jnp.where(low == part, found, 0.0)
    o_ref[0] = total.astype(BF16)


def pick_cols(index, x_train, block=512):
    steps, count = index.shape
    return pl.pallas_call(
        pick_cols_kernel,
        grid=(steps, count // block),
        in_specs=[
            pl.BlockSpec((1, 1, block), lambda t, i: (t, 0, i)),
            pl.BlockSpec(x_train.shape, lambda t, i: (0, 0)),
        ],
        out_specs=pl.BlockSpec((1, x_train.shape[0], block), lambda t, i: (t, 0, i)),
        out_shape=jax.ShapeDtypeStruct((steps, x_train.shape[0], count), BF16),
        compiler_params=pltpu.CompilerParams(vmem_limit_bytes=24 << 20),
        cost_estimate=pl.CostEstimate(
            flops=60 * steps * count * 256, bytes_accessed=1 << 20, transcendentals=0
        ),
        name="pick_cols",
    )(index[:, None, :], x_train)


def spread(index, rows, train):
    high, low = index >> 7, index & 127
    low_hot = (lax.broadcasted_iota(jnp.int32, (128, index.shape[1]), 0) == low).astype(F32).astype(BF16)
    tiles = [jnp.where(high == h, rows, 0.0) for h in range(train // 128)]
    return dot(jnp.concatenate(tiles, axis=0).astype(BF16), low_hot, NT)


def known_kernel(i_ref, t_ref, n_ref, a_ref, v_ref, cnt_ref, a1_ref, a2_ref):
    train = a_ref.shape[1]
    ones = jnp.ones((8, i_ref.shape[1]), F32)
    for t in range(STEPS):
        tiles = spread(i_ref[t : t + 1, :], ones, train)
        for h in range(train // 128):
            cnt_ref[t, :, h * 128 : (h + 1) * 128] = tiles[h * 8 : (h + 1) * 8, :]
    dual, velocity = a_ref[...], v_ref[...]
    fixed = n_ref[...] - t_ref[...]
    for t, out in enumerate((a1_ref, a2_ref)):
        gradient = cnt_ref[t] * (NOISE_VAR * dual + fixed)
        velocity = MOMENTUM * velocity - STEP_SIZE * gradient
        dual = dual + velocity
        out[...] = dual.astype(BF16)


def known_parts(index, targets, noise, dual, velocity):
    shape = dual.shape
    return pl.pallas_call(
        known_kernel,
        out_shape=(
            jax.ShapeDtypeStruct((STEPS,) + shape, F32),
            jax.ShapeDtypeStruct(shape, BF16),
            jax.ShapeDtypeStruct(shape, BF16),
        ),
        compiler_params=pltpu.CompilerParams(vmem_limit_bytes=32 << 20),
        cost_estimate=pl.CostEstimate(flops=1 << 23, bytes_accessed=1 << 20, transcendentals=0),
        name="known_parts",
    )(index, targets[None, :], noise, dual, velocity)


def place_kernel(i_ref, r_ref, o_ref):
    train = o_ref.shape[1]
    tiles = spread(i_ref[...], r_ref[...].astype(F32), train)
    for h in range(train // 128):
        o_ref[:, h * 128 : (h + 1) * 128] = tiles[h * 8 : (h + 1) * 8, :]


def place(index, rows, train):
    return pl.pallas_call(
        place_kernel,
        out_shape=jax.ShapeDtypeStruct((8, train), F32),
        compiler_params=pltpu.CompilerParams(vmem_limit_bytes=32 << 20),
        cost_estimate=pl.CostEstimate(flops=1 << 21, bytes_accessed=1 << 18, transcendentals=0),
        name="place",
    )(index[None, :], rows)


def finish_kernel(i_ref, r_ref, z0_ref, z1_ref, cnt_ref, t_ref, n_ref, a_ref, v_ref, ao_ref, vo_ref):
    train = a_ref.shape[1]
    rows = r_ref[...]
    coarse = rows.astype(BF16).astype(F32)
    tiles = spread(i_ref[...], coarse, train) + spread(i_ref[...], rows - coarse, train)
    dual, velocity = a_ref[...], v_ref[...]
    fixed = n_ref[...] - t_ref[...]
    z0 = z0_ref[...]
    velocity = MOMENTUM * velocity - STEP_SIZE * (z0 + cnt_ref[0] * (NOISE_VAR * dual + fixed))
    first = dual - STEP_SIZE * z0
    known = dual
    dual = dual + velocity
    change = -STEP_SIZE * z0
    gradient = z1_ref[...] + cnt_ref[1] * (NOISE_VAR * (dual - change) + fixed)
    velocity = MOMENTUM * velocity - STEP_SIZE * gradient
    dual = dual + velocity
    base = cnt_ref[2] * (NOISE_VAR * dual + fixed)
    for h in range(train // 128):
        at = slice(h * 128, (h + 1) * 128)
        vo_ref[:, at] = MOMENTUM * velocity[:, at] - STEP_SIZE * (
            base[:, at] + tiles[h * 8 : (h + 1) * 8, :]
        )
    ao_ref[...] = dual + vo_ref[...]


def finish(index, rows, z0, z1, counts, targets, noise, dual, velocity):
    shape = jax.ShapeDtypeStruct(dual.shape, F32)
    return pl.pallas_call(
        finish_kernel,
        out_shape=(shape, shape),
        compiler_params=pltpu.CompilerParams(vmem_limit_bytes=48 << 20),
        cost_estimate=pl.CostEstimate(flops=1 << 22, bytes_accessed=1 << 20, transcendentals=0),
        name="finish",
    )(index[None, :], rows, z0, z1, counts, targets[None, :], noise, dual, velocity)


def row_id_of(x, z, core):
    return (x * 4 + z) * 2 + core


X_GROUPS = [[row_id_of(x, z, c) for x in range(4)] for z in range(4) for c in range(2)]
Z_GROUPS = [[row_id_of(x, z, c) for z in range(4)] for x in range(4) for c in range(2)]
CORE_SWAP = [(i, i ^ 1) for i in range(32)]


def gather_groups(x, groups):
    spread_out = jnp.broadcast_to(x[None], (len(groups[0]),) + x.shape)
    return lax.all_to_all(spread_out, "row", 0, 0, axis_index_groups=groups, tiled=True)


def gather_rows(x, row_id):
    shape = x.shape
    x = gather_groups(x, Z_GROUPS)
    x = gather_groups(x, X_GROUPS)
    other = lax.ppermute(x, "row", CORE_SWAP)
    even = row_id % 2 == 0
    pair = jnp.stack([jnp.where(even, x, other), jnp.where(even, other, x)], axis=2)
    return pair.reshape((32,) + shape)


def shards(
    x_train,
    targets,
    noise_draws,
    alpha_init,
    velocity_init,
    frequencies,
    phases,
    path_weights,
    x_window,
    batch_index,
):
    rows, cols = lax.axis_size("row"), lax.axis_size("col")
    row_id, col_id = lax.axis_index("row"), lax.axis_index("col")
    train = x_train.shape[1]
    batch_rows = batch_index.shape[1] // rows
    own_rows = batch_rows // cols
    group_rows = rows * own_rows
    paths = path_weights.shape[1]
    own_paths = paths // rows
    factor = (2.0 / (frequencies.shape[1] * cols)) ** 0.5
    dual, velocity, noise = alpha_init.T, velocity_init.T, noise_draws.T

    by_group = batch_index.reshape(STEPS, rows, cols, own_rows)
    mine = lax.dynamic_slice_in_dim(by_group, col_id, 1, 2)[:, :, 0] - col_id * train
    group_index = mine.reshape(STEPS, group_rows)
    own_index = lax.dynamic_slice_in_dim(mine, row_id, 1, 1).reshape(STEPS * own_rows)

    own_points = pick_rows(own_index, x_train)
    points = lax.all_to_all(
        jnp.broadcast_to(own_points[None], (cols,) + own_points.shape), "col", 0, 0, tiled=True
    )
    points = points.reshape(cols, STEPS, own_rows, -1).transpose(1, 0, 2, 3)
    points = points.reshape(STEPS, batch_rows, -1)

    gathered0 = gather_rows(dual.astype(BF16), row_id).reshape(paths, train)
    counts, known1, known2 = known_parts(group_index, targets, noise, dual, velocity)
    gathered1 = lax.all_gather(known1, "row", axis=0, tiled=True)
    gathered2 = lax.all_gather(known2, "row", axis=0, tiled=True)

    window_part = window_prior(frequencies, phases, path_weights, x_window, factor)
    prior_window = lax.psum_scatter(window_part, "col", scatter_dimension=0, tiled=True)

    prior = batch_prior(points.reshape(STEPS * batch_rows, -1), frequencies, phases, path_weights, factor)
    prior = prior.reshape(STEPS, batch_rows, paths)
    full = [matern(points[t], x_train) for t in range(STEPS)]
    group_points = pick_cols(group_index[:2], x_train)
    row_index = lax.dynamic_slice_in_dim(batch_index, row_id * batch_rows, batch_rows, 1) - col_id * train
    between10 = matern_same(points[1], group_points[0], row_index[1][:, None], group_index[0][None, :])
    between20 = matern(points[2], group_points[0])
    between21 = matern(points[2], group_points[1])

    def reduce_cols(part):
        blocks = part.astype(BF16).reshape(cols, own_rows, paths)
        blocks = lax.all_to_all(blocks, "col", 0, 0, tiled=True)
        return jnp.sum(blocks.astype(F32), axis=0)

    chooser = lax.broadcasted_iota(jnp.int32, (own_paths, paths), 1)
    chooser = chooser - own_paths * row_id == lax.broadcasted_iota(jnp.int32, (own_paths, paths), 0)
    chooser = chooser.astype(BF16)

    terms0 = reduce_cols(dot(full[0], gathered0, NT) + prior[0]).astype(BF16)
    terms0 = gather_rows(terms0, row_id).reshape(group_rows, paths)
    part1 = dot(full[1], gathered1, NT) + prior[1]
    terms1 = reduce_cols(part1 - STEP_SIZE * dot(between10, terms0)).astype(BF16)
    z0 = place(group_index[0], dot(chooser, terms0, NT), train)
    part2 = dot(full[2], gathered2, NT) + prior[2]
    part2 = part2 - (STEP_SIZE * (1.0 + MOMENTUM)) * dot(between20, terms0)
    terms1 = gather_rows(terms1, row_id).reshape(group_rows, paths)
    terms2 = reduce_cols(part2 - STEP_SIZE * dot(between21, terms1))
    z1 = place(group_index[1], dot(chooser, terms1, NT), train)
    blocks = terms2.T.reshape(rows, own_paths, own_rows)
    blocks = lax.all_to_all(blocks, "row", 0, 0, tiled=True)
    own_terms = blocks.transpose(1, 0, 2).reshape(own_paths, group_rows)
    dual, velocity = finish(
        group_index[2], own_terms, z0, z1, counts, targets, noise, dual, velocity
    )
    return (dual.T, velocity.T, prior_window)


def solution(mesh):
    placed = (
        P(None, "col"),
        P("col"),
        P("col", "row"),
        P("col", "row"),
        P("col", "row"),
        P(None, "col"),
        P("col"),
        P("col", None),
        P(None, "row"),
        P(),
    )
    return jax.shard_map(
        shards,
        mesh=mesh,
        in_specs=placed,
        out_specs=(P("col", "row"), P("col", "row"), P("col", "row")),
        check_vma=False,
    )
```

```python
import jax
import jax.numpy as jnp
import numpy as np
from jax import lax
from jax.experimental import pallas as pl
from jax.experimental.pallas import tpu as pltpu
from jax.sharding import PartitionSpec as P

STEPS = 3
NOISE_VAR = 0.25
MOMENTUM = 0.9
STEP_SIZE = 0.5
LENGTH = 1.15
F32 = jnp.float32
BF16 = jnp.bfloat16
SCALE = float(np.sqrt(3.0) / LENGTH)
LOG2_E = float(1.0 / np.log(2.0))
NN = (((1,), (0,)), ((), ()))
NT = (((1,), (1,)), ((), ()))


def cosine_fit(factor):
    top = 0.2501
    nodes = (np.cos((2 * np.arange(200) + 1) * np.pi / 400) + 1) * top / 2
    wanted = np.sqrt(2.0 * factor) * np.cos(np.pi * np.sqrt(nodes))
    fit = np.polynomial.chebyshev.Chebyshev.fit(nodes, wanted, 5, domain=[0, top])
    return [float(v) for v in fit.convert(kind=np.polynomial.Polynomial).coef]


def dot(a, b, dims=NN):
    return lax.dot_general(a, b, dims, preferred_element_type=F32)


def scaled_cos(half_arg, factor):
    coefs = cosine_fit(factor)
    turns = half_arg * (1.0 / np.pi)
    f = turns - jnp.round(turns)
    z = f * f
    c = z * coefs[-1] + coefs[-2]
    for coef in coefs[-3::-1]:
        c = c * z + coef
    return c * c - factor


def matern_of(dist_sq):
    dist_sq = jnp.maximum(dist_sq, 1e-30)
    dist = dist_sq * lax.rsqrt(dist_sq)
    return (dist * SCALE + 1.0) * jnp.exp2(dist * (-SCALE * LOG2_E))


def three_parts(x):
    high = x.astype(BF16).astype(F32)
    middle = (x - high).astype(BF16).astype(F32)
    return high, middle, x - high - middle


def wide_columns(body, first, second):
    cols = body.shape[1]
    row = lax.broadcasted_iota(jnp.int32, (16, cols), 0)
    high, middle, low = three_parts(second)
    extra = jnp.where(row < 3, first, 0.0)
    extra = jnp.where(row == 3, high, extra)
    extra = jnp.where(row == 4, middle, extra)
    extra = jnp.where(row == 5, low, extra)
    return jnp.concatenate(
        [body.astype(BF16), extra.astype(BF16), jnp.zeros((48, cols), BF16)], axis=0
    )


def distance_columns(b):
    return wide_columns(b * -2.0, 1.0, jnp.sum(b * b, axis=0, keepdims=True))


def setup_kernel(i_ref, x_ref, f_ref, ph_ref, p_ref, xo_ref, fo_ref):
    index = i_ref[...]
    high, low = index & 255, index >> 8
    onehot = (lax.broadcasted_iota(jnp.int32, (index.shape[0], 256), 1) == high).astype(F32).astype(BF16)
    total = jnp.zeros((index.shape[0], x_ref.shape[0]), F32)
    for part in range(x_ref.shape[1] // 256):
        found = dot(onehot, x_ref[:, part * 256 : (part + 1) * 256], NT)
        total = total + jnp.where(low == part, found, 0.0)
    high, middle, low = three_parts(jnp.sum(total * total, axis=1, keepdims=True))
    lane = lax.broadcasted_iota(jnp.int32, total.shape, 1)
    extra = jnp.where(lane < 6, 1.0, 0.0)
    extra = jnp.where(lane == 0, high, extra)
    extra = jnp.where(lane == 1, middle, extra)
    extra = jnp.where(lane == 2, low, extra)
    p_ref[:, :64] = total.astype(BF16)
    p_ref[:, 64:] = extra.astype(BF16)
    for at in range(0, x_ref.shape[1], 512):
        xo_ref[:, at : at + 512] = distance_columns(x_ref[:, at : at + 512].astype(F32))
    fo_ref[...] = wide_columns(f_ref[...].astype(F32) * 0.5, 0.0, ph_ref[...] * 0.5)


def setup(index, x_train, frequencies, phases):
    return pl.pallas_call(
        setup_kernel,
        out_shape=(
            jax.ShapeDtypeStruct((index.shape[0], 128), BF16),
            jax.ShapeDtypeStruct((128, x_train.shape[1]), BF16),
            jax.ShapeDtypeStruct((128, frequencies.shape[1]), BF16),
        ),
        compiler_params=pltpu.CompilerParams(vmem_limit_bytes=24 << 20),
        cost_estimate=pl.CostEstimate(flops=1 << 22, bytes_accessed=2 << 20, transcendentals=0),
        name="setup",
    )(index[:, None], x_train, frequencies, phases[None, :])


def pick_cols_kernel(i_ref, x_ref, o_ref):
    index = i_ref[0]
    high, low = index & 255, index >> 8
    onehot = (lax.broadcasted_iota(jnp.int32, (256, index.shape[1]), 0) == high).astype(F32).astype(BF16)
    parts = x_ref.shape[1] // 256
    stacked = jnp.concatenate([x_ref[:, k * 256 : (k + 1) * 256] for k in range(parts)], axis=0)
    found = dot(stacked, onehot)
    total = jnp.zeros((x_ref.shape[0], index.shape[1]), F32)
    for k in range(parts):
        total = total + jnp.where(low == k, found[k * 64 : (k + 1) * 64], 0.0)
    o_ref[0] = distance_columns(total)


def pick_cols(index, x_train, block=512):
    steps, count = index.shape
    return pl.pallas_call(
        pick_cols_kernel,
        grid=(steps, count // block),
        in_specs=[
            pl.BlockSpec((1, 1, block), lambda t, i: (t, 0, i)),
            pl.BlockSpec(x_train.shape, lambda t, i: (0, 0)),
        ],
        out_specs=pl.BlockSpec((1, 128, block), lambda t, i: (t, 0, i)),
        out_shape=jax.ShapeDtypeStruct((steps, 128, count), BF16),
        compiler_params=pltpu.CompilerParams(vmem_limit_bytes=24 << 20),
        cost_estimate=pl.CostEstimate(
            flops=60 * steps * count * 256, bytes_accessed=1 << 20, transcendentals=0
        ),
        name="pick_cols",
    )(index[:, None, :], x_train)


def pair_kernel(p_ref, b_ref, *refs):
    p = p_ref[...].reshape(-1, 128)
    for at in range(0, b_ref.shape[2], 256):
        value = matern_of(dot(p, b_ref[0, :, at : at + 256]))
        if len(refs) == 3:
            same = refs[0][...] == refs[1][:, at : at + 256]
            value = value + jnp.where(same, NOISE_VAR, 0.0)
        refs[-1][:, at : at + 256] = value.astype(BF16)


def pair_block(points, place, others, other, point_ids=None, other_ids=None, block=512):
    groups, rows, cols = points.shape[0], points.shape[0] * 64, others.shape[2]
    specs = [
        pl.BlockSpec((groups, 64, 128), lambda i: (0, place, 0)),
        pl.BlockSpec((1, 128, block), lambda i: (other, 0, i)),
    ]
    operands = [points, others]
    if point_ids is not None:
        specs += [pl.BlockSpec((rows, 1), lambda i: (0, 0)), pl.BlockSpec((1, block), lambda i: (0, i))]
        operands += [point_ids, other_ids]
    return pl.pallas_call(
        pair_kernel,
        grid=(cols // block,),
        in_specs=specs,
        out_specs=pl.BlockSpec((rows, block), lambda i: (0, i)),
        out_shape=jax.ShapeDtypeStruct((rows, cols), BF16),
        compiler_params=pltpu.CompilerParams(vmem_limit_bytes=24 << 20),
        cost_estimate=pl.CostEstimate(
            flops=12 * rows * cols, bytes_accessed=2 * rows * cols, transcendentals=2 * rows * cols
        ),
        name="pair_block",
    )(*operands)


def part_sums(p, x_ref, a_ref, f_ref, w, factor):
    total = dot(scaled_cos(dot(p, f_ref[...]), factor).astype(BF16), w)
    for at in range(0, x_ref.shape[1], 256):
        values = matern_of(dot(p, x_ref[:, at : at + 256])).astype(BF16)
        total = total + dot(values, a_ref[:, at : at + 256], NT)
    return total


def part_kernel(p_ref, x_ref, a_ref, f_ref, w_ref, o_ref, *, factor):
    total = part_sums(p_ref[...].reshape(-1, 128), x_ref, a_ref, f_ref, w_ref[...], factor)
    first = pl.program_id(0) == 0

    @pl.when(first)
    def _():
        o_ref[...] = total

    @pl.when(jnp.logical_not(first))
    def _():
        o_ref[...] += total


def part_block(points, place, x_wide, dual, f_wide, weights, factor, blocks=4):
    groups, rows, train = points.shape[0], points.shape[0] * 64, x_wide.shape[1]
    feats, paths = weights.shape
    return pl.pallas_call(
        lambda *refs: part_kernel(*refs, factor=factor),
        grid=(blocks,),
        in_specs=[
            pl.BlockSpec((groups, 64, 128), lambda i: (0, place, 0)),
            pl.BlockSpec((128, train // blocks), lambda i: (0, i)),
            pl.BlockSpec((paths, train // blocks), lambda i: (0, i)),
            pl.BlockSpec((128, feats // blocks), lambda i: (0, i)),
            pl.BlockSpec((feats // blocks, paths), lambda i: (i, 0)),
        ],
        out_specs=pl.BlockSpec((rows, paths), lambda i: (0, 0)),
        out_shape=jax.ShapeDtypeStruct((rows, paths), F32),
        compiler_params=pltpu.CompilerParams(vmem_limit_bytes=28 << 20),
        cost_estimate=pl.CostEstimate(
            flops=12 * rows * train, bytes_accessed=4 << 20, transcendentals=2 * rows * train
        ),
        name="part_block",
    )(points, x_wide, dual, f_wide, weights)


def first_kernel(p_ref, x_ref, a_ref, f_ref, w_ref, c_ref, o_ref, sum_ref, *, factor):
    col, row = pl.program_id(0), pl.program_id(1)
    weights = dot(w_ref[...], c_ref[...], NT).astype(BF16)
    total = part_sums(p_ref[...].reshape(-1, 128), x_ref, a_ref, f_ref, weights, factor)
    rows = total.shape[0]
    at = pl.ds(pl.multiple_of(row * rows, rows), rows)

    @pl.when(col == 0)
    def _():
        sum_ref[at, :] = total

    @pl.when(col > 0)
    def _():
        sum_ref[at, :] += total

    @pl.when(col == pl.num_programs(0) - 1)
    def _():
        done = sum_ref[at, :].astype(BF16).reshape(rows // 256, 2, 128, 64)
        for group in range(rows // 256):
            o_ref[group, :, :64] = done[group, 0]
            o_ref[group, :, 64:] = done[group, 1]


def first_block(points, x_wide, dual, f_wide, weights, chooser, factor, blocks=4):
    groups, train = points.shape[0], x_wide.shape[1]
    feats, paths = weights.shape
    some, chunk = dual.shape[0], 2
    return pl.pallas_call(
        lambda *refs: first_kernel(*refs, factor=factor),
        grid=(blocks, groups // chunk),
        in_specs=[
            pl.BlockSpec((chunk, 256, 128), lambda i, j: (j, 0, 0)),
            pl.BlockSpec((128, train // blocks), lambda i, j: (0, i)),
            pl.BlockSpec((some, train // blocks), lambda i, j: (0, i)),
            pl.BlockSpec((128, feats // blocks), lambda i, j: (0, i)),
            pl.BlockSpec((feats // blocks, paths), lambda i, j: (i, 0)),
            pl.BlockSpec((some, paths), lambda i, j: (0, 0)),
        ],
        out_specs=pl.BlockSpec((chunk, 128, 128), lambda i, j: (j, 0, 0)),
        out_shape=jax.ShapeDtypeStruct((groups, 128, 128), BF16),
        scratch_shapes=[pltpu.VMEM((groups * 256, some), F32)],
        compiler_params=pltpu.CompilerParams(vmem_limit_bytes=28 << 20),
        cost_estimate=pl.CostEstimate(
            flops=12 * groups * 256 * train, bytes_accessed=4 << 20, transcendentals=2 * groups * 256 * train
        ),
        name="first_block",
    )(points, x_wide, dual, f_wide, weights, chooser)


def merge_kernel(b_ref, o_ref):
    lane = lax.broadcasted_iota(jnp.int32, (128, 256), 0)
    path = lax.broadcasted_iota(jnp.int32, (128, 256), 1)
    inner = lane & 63
    core, x, own = inner >> 5, (inner >> 3) & 3, inner & 7
    for half in range(2):
        total = jnp.zeros((128, 256), F32)
        for z in range(4):
            to = ((x * 4 + z) * 2 + core) * 8 + own
            move = jnp.where((path == to) & (lane >> 6 == half), 1.0, 0.0).astype(BF16)
            total = total + dot(b_ref[z], move)
        o_ref[half * 128 : (half + 1) * 128, :] = total.astype(BF16)


def merge(blocks):
    return pl.pallas_call(
        merge_kernel, out_shape=jax.ShapeDtypeStruct((256, 256), BF16), name="merge"
    )(blocks)


def window_kernel(f_ref, w_ref, x_ref, o_ref, *, factor):
    cols = x_ref.shape[1]
    row = lax.broadcasted_iota(jnp.int32, (16, cols), 0)
    ones = jnp.where((row >= 3) & (row < 6), 1.0, 0.0).astype(BF16)
    x = jnp.concatenate([x_ref[...], ones, jnp.zeros((48, cols), BF16)], axis=0)
    for at in range(0, cols, 256):
        phi = scaled_cos(dot(f_ref[...], x[:, at : at + 256]), factor).astype(BF16)
        o_ref[:, at : at + 256] = dot(w_ref[...], phi)


def window_prior(f_rows, weights, x_window, factor, block=512):
    feats, paths, window = f_rows.shape[0], weights.shape[1], x_window.shape[1]
    return pl.pallas_call(
        lambda *refs: window_kernel(*refs, factor=factor),
        grid=(window // block,),
        in_specs=[
            pl.BlockSpec((feats, 128), lambda i: (0, 0)),
            pl.BlockSpec((paths, feats), lambda i: (0, 0)),
            pl.BlockSpec((x_window.shape[0], block), lambda i: (0, i)),
        ],
        out_specs=pl.BlockSpec((paths, block), lambda i: (0, i)),
        out_shape=jax.ShapeDtypeStruct((paths, window), F32),
        compiler_params=pltpu.CompilerParams(vmem_limit_bytes=24 << 20),
        cost_estimate=pl.CostEstimate(
            flops=24 * feats * window, bytes_accessed=4 * paths * window, transcendentals=feats * window
        ),
        name="window_prior",
    )(f_rows, weights.T, x_window)


def spread(index, rows, train):
    high, low = index >> 7, index & 127
    low_hot = (lax.broadcasted_iota(jnp.int32, (128, index.shape[1]), 0) == low).astype(F32).astype(BF16)
    tiles = [jnp.where(high == h, rows, 0.0) for h in range(train // 128)]
    return dot(jnp.concatenate(tiles, axis=0).astype(BF16), low_hot, NT)


def known_kernel(i_ref, t_ref, n_ref, a_ref, v_ref, cnt_ref, a1_ref, a2_ref):
    train = a_ref.shape[1]
    ones = jnp.ones((8, i_ref.shape[1]), F32)
    for t in range(STEPS):
        tiles = spread(i_ref[t : t + 1, :], ones, train)
        for h in range(train // 128):
            cnt_ref[t, :, h * 128 : (h + 1) * 128] = tiles[h * 8 : (h + 1) * 8, :]
    dual, velocity = a_ref[...], v_ref[...]
    fixed = n_ref[...] - t_ref[...]
    for t, out in enumerate((a1_ref, a2_ref)):
        gradient = cnt_ref[t] * (NOISE_VAR * dual + fixed)
        velocity = MOMENTUM * velocity - STEP_SIZE * gradient
        dual = dual + velocity
        out[...] = dual.astype(BF16)


def known_parts(index, targets, noise, dual, velocity):
    shape = dual.shape
    return pl.pallas_call(
        known_kernel,
        out_shape=(
            jax.ShapeDtypeStruct((STEPS,) + shape, F32),
            jax.ShapeDtypeStruct(shape, BF16),
            jax.ShapeDtypeStruct(shape, BF16),
        ),
        compiler_params=pltpu.CompilerParams(vmem_limit_bytes=32 << 20),
        cost_estimate=pl.CostEstimate(flops=1 << 23, bytes_accessed=1 << 20, transcendentals=0),
        name="known_parts",
    )(index, targets[None, :], noise, dual, velocity)


def place_kernel(i_ref, r_ref, o_ref):
    train = o_ref.shape[1]
    tiles = spread(i_ref[...], r_ref[...].astype(F32), train)
    for h in range(train // 128):
        o_ref[:, h * 128 : (h + 1) * 128] = tiles[h * 8 : (h + 1) * 8, :]


def place(index, rows, train):
    return pl.pallas_call(
        place_kernel,
        out_shape=jax.ShapeDtypeStruct((8, train), F32),
        compiler_params=pltpu.CompilerParams(vmem_limit_bytes=32 << 20),
        cost_estimate=pl.CostEstimate(flops=1 << 21, bytes_accessed=1 << 18, transcendentals=0),
        name="place",
    )(index[None, :], rows)


def finish_kernel(i_ref, r_ref, z0_ref, z1_ref, cnt_ref, t_ref, n_ref, a_ref, v_ref, ao_ref, vo_ref):
    train = a_ref.shape[1]
    rows = r_ref[...]
    coarse = rows.astype(BF16).astype(F32)
    tiles = spread(i_ref[...], coarse, train) + spread(i_ref[...], rows - coarse, train)
    dual, velocity = a_ref[...], v_ref[...]
    fixed = n_ref[...] - t_ref[...]
    z0 = z0_ref[...]
    velocity = MOMENTUM * velocity - STEP_SIZE * (z0 + cnt_ref[0] * (NOISE_VAR * dual + fixed))
    first = dual - STEP_SIZE * z0
    known = dual
    dual = dual + velocity
    change = -STEP_SIZE * z0
    gradient = z1_ref[...] + cnt_ref[1] * (NOISE_VAR * (dual - change) + fixed)
    velocity = MOMENTUM * velocity - STEP_SIZE * gradient
    dual = dual + velocity
    base = cnt_ref[2] * (NOISE_VAR * dual + fixed)
    for h in range(train // 128):
        at = slice(h * 128, (h + 1) * 128)
        vo_ref[:, at] = MOMENTUM * velocity[:, at] - STEP_SIZE * (
            base[:, at] + tiles[h * 8 : (h + 1) * 8, :]
        )
    ao_ref[...] = dual + vo_ref[...]


def finish(index, rows, z0, z1, counts, targets, noise, dual, velocity):
    shape = jax.ShapeDtypeStruct(dual.shape, F32)
    return pl.pallas_call(
        finish_kernel,
        out_shape=(shape, shape),
        compiler_params=pltpu.CompilerParams(vmem_limit_bytes=48 << 20),
        cost_estimate=pl.CostEstimate(flops=1 << 22, bytes_accessed=1 << 20, transcendentals=0),
        name="finish",
    )(index[None, :], rows, z0, z1, counts, targets[None, :], noise, dual, velocity)


def row_id_of(x, z, core):
    return (x * 4 + z) * 2 + core


X_GROUPS = [[row_id_of(x, z, c) for x in range(4)] for z in range(4) for c in range(2)]
Z_GROUPS = [[row_id_of(x, z, c) for z in range(4)] for x in range(4) for c in range(2)]
CORE_SWAP = [(i, i ^ 1) for i in range(32)]


def gather_groups(x, groups):
    spread_out = jnp.broadcast_to(x[None], (len(groups[0]),) + x.shape)
    return lax.all_to_all(spread_out, "row", 0, 0, axis_index_groups=groups, tiled=True)


def gather_core(x, row_id):
    other = lax.ppermute(x, "row", CORE_SWAP)
    even = row_id % 2 == 0
    return jnp.concatenate([jnp.where(even, x, other), jnp.where(even, other, x)], axis=0)


def after(*values):
    return lax.optimization_barrier(values)


def shards(
    x_train,
    targets,
    noise_draws,
    alpha_init,
    velocity_init,
    frequencies,
    phases,
    path_weights,
    x_window,
    batch_index,
):
    rows, cols = lax.axis_size("row"), lax.axis_size("col")
    row_id, col_id = lax.axis_index("row"), lax.axis_index("col")
    train = x_train.shape[1]
    batch_rows = batch_index.shape[1] // rows
    own_rows = batch_rows // cols
    group_rows = rows * own_rows
    paths = path_weights.shape[1]
    own_paths = paths // rows
    factor = (2.0 / (frequencies.shape[1] * cols)) ** 0.5
    dual, velocity, noise = alpha_init.T, velocity_init.T, noise_draws.T
    x_id, z_id, core_id = row_id // 8, row_id // 2 % 4, row_id % 2

    by_group = batch_index.reshape(STEPS, rows, cols, own_rows)
    mine = lax.dynamic_slice_in_dim(by_group, col_id, 1, 2)[:, :, 0] - col_id * train
    group_index = mine.reshape(STEPS, group_rows)
    by_place = mine.reshape(STEPS, 4, 4, 2, own_rows)
    sorted_index = by_place[:2].transpose(0, 3, 1, 2, 4).reshape(2, group_rows)
    near = lax.dynamic_slice(by_place[0], (x_id, 0, core_id, 0), (1, 4, 1, own_rows)).reshape(-1)
    own_index = lax.dynamic_slice_in_dim(mine[1:], row_id, 1, 1).reshape(-1)
    own_index = jnp.concatenate([near, own_index])

    gathered0 = gather_groups(dual.astype(BF16), X_GROUPS)
    own_points, x_wide, f_wide = setup(own_index, x_train, frequencies, phases)
    counts, known1, known2 = known_parts(group_index, targets, noise, dual, velocity)
    gathered0, own_points, counts, known1, known2 = after(gathered0, own_points, counts, known1, known2)
    gathered1 = lax.all_gather(known1, "row", axis=0, tiled=True)
    gathered2 = lax.all_gather(known2, "row", axis=0, tiled=True)
    points = lax.all_to_all(
        jnp.broadcast_to(own_points[None], (cols,) + own_points.shape), "col", 0, 0, tiled=True
    )
    gathered0 = gather_core(gathered0, row_id).reshape(paths // 4, train)
    window_part = window_prior(f_wide.T, path_weights, x_window, factor)
    points, window_part, gathered0 = after(points, window_part, gathered0)
    prior_window = lax.psum_scatter(window_part, "col", scatter_dimension=0, tiled=True)

    here = lax.broadcasted_iota(jnp.int32, (paths // 4, paths), 0)
    here = (((here >> 3) % 4 * 4 + z_id) * 2 + (here >> 5)) * own_paths + here % own_paths
    here = (lax.broadcasted_iota(jnp.int32, (paths // 4, paths), 1) == here).astype(BF16)
    blocks = first_block(points, x_wide, gathered0, f_wide, path_weights, here, factor)
    row_index = lax.dynamic_slice_in_dim(batch_index[1], row_id * batch_rows, batch_rows, 0) - col_id * train

    def send_cols(part):
        return lax.all_to_all(part.astype(BF16).reshape(cols, own_rows, paths), "col", 0, 0, tiled=True)

    def add_up(blocks):
        return jnp.sum(blocks.astype(F32), axis=0)

    chooser = lax.broadcasted_iota(jnp.int32, (own_paths, paths), 1)
    chooser = chooser - own_paths * row_id == lax.broadcasted_iota(jnp.int32, (own_paths, paths), 0)
    chooser = chooser.astype(BF16)

    blocks = lax.all_to_all(blocks, "col", 0, 0, tiled=True)
    group_points = pick_cols(sorted_index, x_train)
    blocks, group_points = after(blocks, group_points)
    terms0 = gather_groups(add_up(blocks).astype(BF16), Z_GROUPS)
    between10 = pair_block(points, 4, group_points, 0, row_index[:, None], sorted_index[:1])
    between20 = pair_block(points, 5, group_points, 0)
    terms0, between10, between20 = after(terms0, between10, between20)
    terms0 = gather_groups(merge(terms0), X_GROUPS)
    part1 = part_block(points, 4, x_wide, gathered1, f_wide, path_weights, factor)
    terms0, part1 = after(terms0, part1)
    terms0 = gather_core(terms0, row_id).reshape(group_rows, paths)

    blocks = send_cols(part1 - STEP_SIZE * dot(between10, terms0))
    between21 = pair_block(points, 5, group_points, 1)
    blocks, between21 = after(blocks, between21)
    terms1 = gather_groups(add_up(blocks).astype(BF16), Z_GROUPS)
    part2 = part_block(points, 5, x_wide, gathered2, f_wide, path_weights, factor)
    terms1, part2 = after(terms1, part2)
    terms1 = gather_groups(terms1, X_GROUPS)
    part2 = part2 - (STEP_SIZE * (1.0 + MOMENTUM)) * dot(between20, terms0)
    terms1, part2 = after(terms1, part2)
    terms1 = gather_core(terms1, row_id).reshape(group_rows, paths)

    blocks = send_cols(part2 - STEP_SIZE * dot(between21, terms1))
    z0 = place(sorted_index[0], dot(chooser, terms0, NT), train)
    blocks, z0 = after(blocks, z0)
    blocks = lax.all_to_all(add_up(blocks).T.reshape(rows, own_paths, own_rows), "row", 0, 0, tiled=True)
    z1 = place(sorted_index[1], dot(chooser, terms1, NT), train)
    blocks, z1 = after(blocks, z1)
    own_terms = blocks.transpose(1, 0, 2).reshape(own_paths, group_rows)
    dual, velocity = finish(
        group_index[2], own_terms, z0, z1, counts, targets, noise, dual, velocity
    )
    return (dual.T, velocity.T, prior_window)


def solution(mesh):
    placed = (
        P(None, "col"),
        P("col"),
        P("col", "row"),
        P("col", "row"),
        P("col", "row"),
        P(None, "col"),
        P("col"),
        P("col", None),
        P(None, "row"),
        P(),
    )
    return jax.shard_map(
        shards,
        mesh=mesh,
        in_specs=placed,
        out_specs=(P("col", "row"), P("col", "row"), P("col", "row")),
        check_vma=False,
    )
```

```python
import jax
import jax.numpy as jnp
import numpy as np
from jax import lax
from jax.experimental import pallas as pl
from jax.experimental.pallas import tpu as pltpu
from jax.sharding import PartitionSpec as P

STEPS = 3
NOISE_VAR = 0.25
MOMENTUM = 0.9
STEP_SIZE = 0.5
LENGTH = 1.15
F32 = jnp.float32
BF16 = jnp.bfloat16
SCALE = float(np.sqrt(3.0) / LENGTH)
LOG2_E = float(1.0 / np.log(2.0))
NN = (((1,), (0,)), ((), ()))
NT = (((1,), (1,)), ((), ()))


def cosine_fit(factor):
    top = 0.2501
    nodes = (np.cos((2 * np.arange(200) + 1) * np.pi / 400) + 1) * top / 2
    wanted = np.sqrt(2.0 * factor) * np.cos(np.pi * np.sqrt(nodes))
    fit = np.polynomial.chebyshev.Chebyshev.fit(nodes, wanted, 5, domain=[0, top])
    return [float(v) for v in fit.convert(kind=np.polynomial.Polynomial).coef]


def dot(a, b, dims=NN):
    return lax.dot_general(a, b, dims, preferred_element_type=F32)


def scaled_cos(half_arg, factor):
    coefs = cosine_fit(factor)
    turns = half_arg * (1.0 / np.pi)
    f = turns - jnp.round(turns)
    z = f * f
    c = z * coefs[-1] + coefs[-2]
    for coef in coefs[-3::-1]:
        c = c * z + coef
    return c * c - factor


def matern_of(dist_sq):
    dist_sq = jnp.maximum(dist_sq, 1e-30)
    dist = dist_sq * lax.rsqrt(dist_sq)
    return (dist * SCALE + 1.0) * jnp.exp2(dist * (-SCALE * LOG2_E))


def three_parts(x):
    high = x.astype(BF16).astype(F32)
    middle = (x - high).astype(BF16).astype(F32)
    return high, middle, x - high - middle


def wide_columns(body, first, second):
    cols = body.shape[1]
    row = lax.broadcasted_iota(jnp.int32, (16, cols), 0)
    high, middle, low = three_parts(second)
    extra = jnp.where(row < 3, first, 0.0)
    extra = jnp.where(row == 3, high, extra)
    extra = jnp.where(row == 4, middle, extra)
    extra = jnp.where(row == 5, low, extra)
    return jnp.concatenate(
        [body.astype(BF16), extra.astype(BF16), jnp.zeros((48, cols), BF16)], axis=0
    )


def distance_columns(b):
    return wide_columns(b * -2.0, 1.0, jnp.sum(b * b, axis=0, keepdims=True))


def setup_kernel(i_ref, x_ref, f_ref, ph_ref, p_ref, xo_ref, fo_ref):
    index = i_ref[...]
    high, low = index & 255, index >> 8
    onehot = (lax.broadcasted_iota(jnp.int32, (index.shape[0], 256), 1) == high).astype(F32).astype(BF16)
    total = jnp.zeros((index.shape[0], x_ref.shape[0]), F32)
    for part in range(x_ref.shape[1] // 256):
        found = dot(onehot, x_ref[:, part * 256 : (part + 1) * 256], NT)
        total = total + jnp.where(low == part, found, 0.0)
    high, middle, low = three_parts(jnp.sum(total * total, axis=1, keepdims=True))
    lane = lax.broadcasted_iota(jnp.int32, total.shape, 1)
    extra = jnp.where(lane < 6, 1.0, 0.0)
    extra = jnp.where(lane == 0, high, extra)
    extra = jnp.where(lane == 1, middle, extra)
    extra = jnp.where(lane == 2, low, extra)
    p_ref[:, :64] = total.astype(BF16)
    p_ref[:, 64:] = extra.astype(BF16)
    for at in range(0, x_ref.shape[1], 512):
        xo_ref[:, at : at + 512] = distance_columns(x_ref[:, at : at + 512].astype(F32))
    fo_ref[...] = wide_columns(f_ref[...].astype(F32) * 0.5, 0.0, ph_ref[...] * 0.5)


def setup(index, x_train, frequencies, phases):
    return pl.pallas_call(
        setup_kernel,
        out_shape=(
            jax.ShapeDtypeStruct((index.shape[0], 128), BF16),
            jax.ShapeDtypeStruct((128, x_train.shape[1]), BF16),
            jax.ShapeDtypeStruct((128, frequencies.shape[1]), BF16),
        ),
        compiler_params=pltpu.CompilerParams(vmem_limit_bytes=24 << 20),
        cost_estimate=pl.CostEstimate(flops=1 << 22, bytes_accessed=2 << 20, transcendentals=0),
        name="setup",
    )(index[:, None], x_train, frequencies, phases[None, :])


def pick_cols_kernel(i_ref, x_ref, o_ref):
    index = i_ref[0]
    high, low = index & 255, index >> 8
    onehot = (lax.broadcasted_iota(jnp.int32, (256, index.shape[1]), 0) == high).astype(F32).astype(BF16)
    parts = x_ref.shape[1] // 256
    stacked = jnp.concatenate([x_ref[:, k * 256 : (k + 1) * 256] for k in range(parts)], axis=0)
    found = dot(stacked, onehot)
    total = jnp.zeros((x_ref.shape[0], index.shape[1]), F32)
    for k in range(parts):
        total = total + jnp.where(low == k, found[k * 64 : (k + 1) * 64], 0.0)
    o_ref[0] = distance_columns(total)


def pick_cols(index, x_train, block=512):
    steps, count = index.shape
    return pl.pallas_call(
        pick_cols_kernel,
        grid=(steps, count // block),
        in_specs=[
            pl.BlockSpec((1, 1, block), lambda t, i: (t, 0, i)),
            pl.BlockSpec(x_train.shape, lambda t, i: (0, 0)),
        ],
        out_specs=pl.BlockSpec((1, 128, block), lambda t, i: (t, 0, i)),
        out_shape=jax.ShapeDtypeStruct((steps, 128, count), BF16),
        compiler_params=pltpu.CompilerParams(vmem_limit_bytes=24 << 20),
        cost_estimate=pl.CostEstimate(
            flops=60 * steps * count * 256, bytes_accessed=1 << 20, transcendentals=0
        ),
        name="pick_cols",
    )(index[:, None, :], x_train)


def pair_kernel(p_ref, b_ref, *refs):
    p = p_ref[...].reshape(-1, 128)
    for at in range(0, b_ref.shape[2], 256):
        value = matern_of(dot(p, b_ref[0, :, at : at + 256]))
        if len(refs) == 3:
            same = refs[0][...] == refs[1][:, at : at + 256]
            value = value + jnp.where(same, NOISE_VAR, 0.0)
        refs[-1][:, at : at + 256] = value.astype(BF16)


def pair_block(points, place, others, other, point_ids=None, other_ids=None, block=1024):
    groups, rows, cols = points.shape[0], points.shape[0] * 64, others.shape[2]
    specs = [
        pl.BlockSpec((groups, 64, 128), lambda i: (0, place, 0)),
        pl.BlockSpec((1, 128, block), lambda i: (other, 0, i)),
    ]
    operands = [points, others]
    if point_ids is not None:
        specs += [pl.BlockSpec((rows, 1), lambda i: (0, 0)), pl.BlockSpec((1, block), lambda i: (0, i))]
        operands += [point_ids, other_ids]
    return pl.pallas_call(
        pair_kernel,
        grid=(cols // block,),
        in_specs=specs,
        out_specs=pl.BlockSpec((rows, block), lambda i: (0, i)),
        out_shape=jax.ShapeDtypeStruct((rows, cols), BF16),
        compiler_params=pltpu.CompilerParams(vmem_limit_bytes=24 << 20),
        cost_estimate=pl.CostEstimate(
            flops=12 * rows * cols, bytes_accessed=2 * rows * cols, transcendentals=2 * rows * cols
        ),
        name="pair_block",
    )(*operands)


def part_sums(p, x_ref, a_ref, f_ref, w, factor):
    total = dot(scaled_cos(dot(p, f_ref[...]), factor).astype(BF16), w)
    for at in range(0, x_ref.shape[1], 256):
        values = matern_of(dot(p, x_ref[:, at : at + 256])).astype(BF16)
        total = total + dot(values, a_ref[:, at : at + 256], NT)
    return total


def part_kernel(p_ref, x_ref, a_ref, f_ref, w_ref, o_ref, *, factor):
    total = part_sums(p_ref[...].reshape(-1, 128), x_ref, a_ref, f_ref, w_ref[...], factor)
    first = pl.program_id(0) == 0

    @pl.when(first)
    def _():
        o_ref[...] = total

    @pl.when(jnp.logical_not(first))
    def _():
        o_ref[...] += total


def part_block(points, place, x_wide, dual, f_wide, weights, factor, blocks=2):
    groups, rows, train = points.shape[0], points.shape[0] * 64, x_wide.shape[1]
    feats, paths = weights.shape
    return pl.pallas_call(
        lambda *refs: part_kernel(*refs, factor=factor),
        grid=(blocks,),
        in_specs=[
            pl.BlockSpec((groups, 64, 128), lambda i: (0, place, 0)),
            pl.BlockSpec((128, train // blocks), lambda i: (0, i)),
            pl.BlockSpec((paths, train // blocks), lambda i: (0, i)),
            pl.BlockSpec((128, feats // blocks), lambda i: (0, i)),
            pl.BlockSpec((feats // blocks, paths), lambda i: (i, 0)),
        ],
        out_specs=pl.BlockSpec((rows, paths), lambda i: (0, 0)),
        out_shape=jax.ShapeDtypeStruct((rows, paths), F32),
        compiler_params=pltpu.CompilerParams(vmem_limit_bytes=28 << 20),
        cost_estimate=pl.CostEstimate(
            flops=12 * rows * train, bytes_accessed=4 << 20, transcendentals=2 * rows * train
        ),
        name="part_block",
    )(points, x_wide, dual, f_wide, weights)


def first_kernel(p_ref, x_ref, a_ref, f_ref, w_ref, c_ref, o_ref, sum_ref, *, factor):
    col, row = pl.program_id(0), pl.program_id(1)
    weights = dot(w_ref[...], c_ref[...], NT).astype(BF16)
    total = part_sums(p_ref[...].reshape(-1, 128), x_ref, a_ref, f_ref, weights, factor)
    rows = total.shape[0]
    at = pl.ds(pl.multiple_of(row * rows, rows), rows)

    @pl.when(col == 0)
    def _():
        sum_ref[at, :] = total

    @pl.when(col > 0)
    def _():
        sum_ref[at, :] += total

    @pl.when(col == pl.num_programs(0) - 1)
    def _():
        done = sum_ref[at, :].astype(BF16).reshape(rows // 256, 2, 128, 64)
        for group in range(rows // 256):
            o_ref[group, :, :64] = done[group, 0]
            o_ref[group, :, 64:] = done[group, 1]


def first_block(points, x_wide, dual, f_wide, weights, chooser, factor, blocks=2):
    groups, train = points.shape[0], x_wide.shape[1]
    feats, paths = weights.shape
    some, chunk = dual.shape[0], 4
    return pl.pallas_call(
        lambda *refs: first_kernel(*refs, factor=factor),
        grid=(blocks, groups // chunk),
        in_specs=[
            pl.BlockSpec((chunk, 256, 128), lambda i, j: (j, 0, 0)),
            pl.BlockSpec((128, train // blocks), lambda i, j: (0, i)),
            pl.BlockSpec((some, train // blocks), lambda i, j: (0, i)),
            pl.BlockSpec((128, feats // blocks), lambda i, j: (0, i)),
            pl.BlockSpec((feats // blocks, paths), lambda i, j: (i, 0)),
            pl.BlockSpec((some, paths), lambda i, j: (0, 0)),
        ],
        out_specs=pl.BlockSpec((chunk, 128, 128), lambda i, j: (j, 0, 0)),
        out_shape=jax.ShapeDtypeStruct((groups, 128, 128), BF16),
        scratch_shapes=[pltpu.VMEM((groups * 256, some), F32)],
        compiler_params=pltpu.CompilerParams(vmem_limit_bytes=28 << 20),
        cost_estimate=pl.CostEstimate(
            flops=12 * groups * 256 * train, bytes_accessed=4 << 20, transcendentals=2 * groups * 256 * train
        ),
        name="first_block",
    )(points, x_wide, dual, f_wide, weights, chooser)


def merge_kernel(to_ref, b0_ref, b1_ref, b2_ref, b3_ref, o_ref):
    lane = lax.broadcasted_iota(jnp.int32, (128, 256), 0)
    path = lax.broadcasted_iota(jnp.int32, (128, 256), 1)
    for half in range(2):
        total = jnp.zeros((128, 256), F32)
        for k, b_ref in enumerate((b0_ref, b1_ref, b2_ref, b3_ref)):
            found = (path == to_ref[:, k : k + 1]) & (lane >> 6 == half)
            total = total + dot(b_ref[...], jnp.where(found, 1.0, 0.0).astype(BF16))
        o_ref[half * 128 : (half + 1) * 128, :] = total.astype(BF16)


def merge(to, blocks):
    return pl.pallas_call(
        merge_kernel, out_shape=jax.ShapeDtypeStruct((256, 256), BF16), name="merge"
    )(to, *blocks)


def chain_kernel(part_ref, k_ref, *refs):
    total = part_ref[...]
    cols = refs[0].shape[0]
    for i, r_ref in enumerate(refs[:-1]):
        total = total - STEP_SIZE * dot(k_ref[:, i * cols : (i + 1) * cols], r_ref[...])
    refs[-1][...] = total.astype(BF16)


def chain(part, block, pieces):
    return pl.pallas_call(
        chain_kernel,
        out_shape=jax.ShapeDtypeStruct(part.shape, BF16),
        compiler_params=pltpu.CompilerParams(vmem_limit_bytes=16 << 20),
        cost_estimate=pl.CostEstimate(flops=1 << 29, bytes_accessed=4 << 20, transcendentals=0),
        name="chain",
    )(part, block, *pieces)


def last_kernel(part_ref, k_ref, *refs):
    total = part_ref[...]
    cols = refs[0].shape[0]
    for i, r_ref in enumerate(refs[:-1]):
        total = total - STEP_SIZE * dot(k_ref[:, i * cols : (i + 1) * cols], r_ref[...])
    turned = total.T
    o_ref = refs[-1]
    for c in range(o_ref.shape[1]):
        o_ref[:, c] = turned[:, c * 64 : (c + 1) * 64].reshape(o_ref.shape[0], 8, 64).astype(BF16)


def last(part, block, pieces):
    rows, paths = part.shape
    return pl.pallas_call(
        last_kernel,
        out_shape=jax.ShapeDtypeStruct((paths // 8, rows // 64, 8, 64), BF16),
        compiler_params=pltpu.CompilerParams(vmem_limit_bytes=16 << 20),
        cost_estimate=pl.CostEstimate(flops=1 << 29, bytes_accessed=4 << 20, transcendentals=0),
        name="last",
    )(part, block, *pieces)


def fold_kernel(part_ref, p_ref, b_ref, *refs):
    p = p_ref[...].reshape(-1, 128)
    total = part_ref[...]
    cols = refs[0].shape[0]
    for i, r_ref in enumerate(refs[:-1]):
        values = matern_of(dot(p, b_ref[0, :, i * cols : (i + 1) * cols])).astype(BF16)
        total = total - (STEP_SIZE * (1.0 + MOMENTUM)) * dot(values, r_ref[...])
    refs[-1][...] = total


def fold(part, points, place, others, other, pieces):
    whole = pl.BlockSpec(part.shape, lambda i: (0, 0))
    piece = pl.BlockSpec(pieces[0].shape, lambda i: (0, 0))
    return pl.pallas_call(
        fold_kernel,
        grid=(1,),
        in_specs=[
            whole,
            pl.BlockSpec((points.shape[0], 64, 128), lambda i: (0, place, 0)),
            pl.BlockSpec((1,) + others.shape[1:], lambda i: (other, 0, 0)),
        ]
        + [piece] * len(pieces),
        out_specs=whole,
        out_shape=jax.ShapeDtypeStruct(part.shape, F32),
        compiler_params=pltpu.CompilerParams(vmem_limit_bytes=24 << 20),
        cost_estimate=pl.CostEstimate(flops=1 << 29, bytes_accessed=4 << 20, transcendentals=1 << 21),
        name="fold",
    )(part, points, others, *pieces)


def window_kernel(f_ref, w_ref, x_ref, o_ref, *, factor):
    cols = x_ref.shape[1]
    row = lax.broadcasted_iota(jnp.int32, (16, cols), 0)
    ones = jnp.where((row >= 3) & (row < 6), 1.0, 0.0).astype(BF16)
    x = jnp.concatenate([x_ref[...], ones, jnp.zeros((48, cols), BF16)], axis=0)
    for at in range(0, cols, 256):
        phi = scaled_cos(dot(f_ref[...], x[:, at : at + 256]), factor).astype(BF16)
        o_ref[:, at : at + 256] = dot(w_ref[...], phi)


def window_prior(f_rows, weights, x_window, factor, block=1024):
    feats, paths, window = f_rows.shape[0], weights.shape[1], x_window.shape[1]
    return pl.pallas_call(
        lambda *refs: window_kernel(*refs, factor=factor),
        grid=(window // block,),
        in_specs=[
            pl.BlockSpec((feats, 128), lambda i: (0, 0)),
            pl.BlockSpec((paths, feats), lambda i: (0, 0)),
            pl.BlockSpec((x_window.shape[0], block), lambda i: (0, i)),
        ],
        out_specs=pl.BlockSpec((paths, block), lambda i: (0, i)),
        out_shape=jax.ShapeDtypeStruct((paths, window), F32),
        compiler_params=pltpu.CompilerParams(vmem_limit_bytes=24 << 20),
        cost_estimate=pl.CostEstimate(
            flops=24 * feats * window, bytes_accessed=4 * paths * window, transcendentals=feats * window
        ),
        name="window_prior",
    )(f_rows, weights.T, x_window)


def spread(index, rows, train):
    high, low = index >> 7, index & 127
    low_hot = (lax.broadcasted_iota(jnp.int32, (128, index.shape[1]), 0) == low).astype(F32).astype(BF16)
    tiles = [jnp.where(high == h, rows, 0.0) for h in range(train // 128)]
    return dot(jnp.concatenate(tiles, axis=0).astype(BF16), low_hot, NT)


def known_kernel(i_ref, t_ref, n_ref, a_ref, v_ref, cnt_ref, a1_ref, a2_ref):
    train = a_ref.shape[1]
    ones = jnp.ones((8, i_ref.shape[1]), F32)
    for t in range(STEPS):
        tiles = spread(i_ref[t : t + 1, :], ones, train)
        for h in range(train // 128):
            cnt_ref[t, :, h * 128 : (h + 1) * 128] = tiles[h * 8 : (h + 1) * 8, :]
    dual, velocity = a_ref[...], v_ref[...]
    fixed = n_ref[...] - t_ref[...]
    for t, out in enumerate((a1_ref, a2_ref)):
        gradient = cnt_ref[t] * (NOISE_VAR * dual + fixed)
        velocity = MOMENTUM * velocity - STEP_SIZE * gradient
        dual = dual + velocity
        out[...] = dual.astype(BF16)


def known_parts(index, targets, noise, dual, velocity):
    shape = dual.shape
    return pl.pallas_call(
        known_kernel,
        out_shape=(
            jax.ShapeDtypeStruct((STEPS,) + shape, F32),
            jax.ShapeDtypeStruct(shape, BF16),
            jax.ShapeDtypeStruct(shape, BF16),
        ),
        compiler_params=pltpu.CompilerParams(vmem_limit_bytes=32 << 20),
        cost_estimate=pl.CostEstimate(flops=1 << 23, bytes_accessed=1 << 20, transcendentals=0),
        name="known_parts",
    )(index, targets[None, :], noise, dual, velocity)


def place_kernel(i_ref, c_ref, *refs):
    o_ref = refs[-1]
    train = o_ref.shape[1]
    rows = jnp.concatenate([dot(c_ref[...], r_ref[...], NT) for r_ref in refs[:-1]], axis=1)
    tiles = spread(i_ref[...], rows, train)
    for h in range(train // 128):
        o_ref[:, h * 128 : (h + 1) * 128] = tiles[h * 8 : (h + 1) * 8, :]


def place(index, chooser, pieces, train):
    return pl.pallas_call(
        place_kernel,
        out_shape=jax.ShapeDtypeStruct((8, train), F32),
        compiler_params=pltpu.CompilerParams(vmem_limit_bytes=32 << 20),
        cost_estimate=pl.CostEstimate(flops=1 << 22, bytes_accessed=1 << 20, transcendentals=0),
        name="place",
    )(index[None, :], chooser, *pieces)


def finish_kernel(i_ref, r_ref, z0_ref, z1_ref, cnt_ref, t_ref, n_ref, a_ref, v_ref, ao_ref, vo_ref, rows_ref):
    train = a_ref.shape[1]
    for r in range(r_ref.shape[0]):
        rows_ref[:, r * 64 : (r + 1) * 64] = jnp.sum(r_ref[r].astype(F32), axis=0)
    rows = rows_ref[...]
    coarse = rows.astype(BF16).astype(F32)
    tiles = spread(i_ref[...], coarse, train) + spread(i_ref[...], rows - coarse, train)
    dual, velocity = a_ref[...], v_ref[...]
    fixed = n_ref[...] - t_ref[...]
    z0 = z0_ref[...]
    velocity = MOMENTUM * velocity - STEP_SIZE * (z0 + cnt_ref[0] * (NOISE_VAR * dual + fixed))
    dual = dual + velocity
    change = -STEP_SIZE * z0
    gradient = z1_ref[...] + cnt_ref[1] * (NOISE_VAR * (dual - change) + fixed)
    velocity = MOMENTUM * velocity - STEP_SIZE * gradient
    dual = dual + velocity
    base = cnt_ref[2] * (NOISE_VAR * dual + fixed)
    for h in range(train // 128):
        at = slice(h * 128, (h + 1) * 128)
        vo_ref[:, at] = MOMENTUM * velocity[:, at] - STEP_SIZE * (
            base[:, at] + tiles[h * 8 : (h + 1) * 8, :]
        )
    ao_ref[...] = dual + vo_ref[...]


def finish(index, rows, z0, z1, counts, targets, noise, dual, velocity):
    shape = jax.ShapeDtypeStruct(dual.shape, F32)
    return pl.pallas_call(
        finish_kernel,
        out_shape=(shape, shape),
        scratch_shapes=[pltpu.VMEM((8, rows.shape[0] * 64), F32)],
        compiler_params=pltpu.CompilerParams(vmem_limit_bytes=48 << 20),
        cost_estimate=pl.CostEstimate(flops=1 << 22, bytes_accessed=1 << 20, transcendentals=0),
        name="finish",
    )(index[None, :], rows, z0, z1, counts, targets[None, :], noise, dual, velocity)


def row_moves(dx, dz, dcore):
    return [
        ((x * 4 + z) * 2 + core, ((x + dx) % 4 * 4 + (z + dz) % 4) * 2 + (core ^ dcore))
        for x in range(4)
        for z in range(4)
        for core in range(2)
    ]


def from_x(block):
    return [block] + [lax.ppermute(block, "row", row_moves(d, 0, 0)) for d in (1, 2, 3)]


def from_z(block):
    return [block] + [lax.ppermute(block, "row", row_moves(0, d, 0)) for d in (1, 2, 3)]


def with_other_core(blocks):
    return blocks + [lax.ppermute(block, "row", row_moves(0, 0, 1)) for block in blocks]


def back_from(array, here, axis):
    turned = jnp.flip(array, axis)
    return lax.dynamic_slice_in_dim(jnp.concatenate([turned, turned], axis), 3 - here, 4, axis)


def after(*values):
    return lax.optimization_barrier(values)


def shards(
    x_train,
    targets,
    noise_draws,
    alpha_init,
    velocity_init,
    frequencies,
    phases,
    path_weights,
    x_window,
    batch_index,
):
    rows, cols = lax.axis_size("row"), lax.axis_size("col")
    row_id, col_id = lax.axis_index("row"), lax.axis_index("col")
    train = x_train.shape[1]
    batch_rows = batch_index.shape[1] // rows
    own_rows = batch_rows // cols
    group_rows = rows * own_rows
    paths = path_weights.shape[1]
    own_paths = paths // rows
    factor = (2.0 / (frequencies.shape[1] * cols)) ** 0.5
    dual, velocity, noise = alpha_init.T, velocity_init.T, noise_draws.T
    x_id, z_id, core_id = row_id // 8, row_id // 2 % 4, row_id % 2

    by_group = batch_index.reshape(STEPS, rows, cols, own_rows)
    mine = lax.dynamic_slice_in_dim(by_group, col_id, 1, 2)[:, :, 0] - col_id * train
    by_place = mine.reshape(STEPS, 4, 4, 2, own_rows)
    near = lax.dynamic_slice(by_place[0], (x_id, 0, core_id, 0), (1, 4, 1, own_rows)).reshape(-1)
    own_index = lax.dynamic_slice_in_dim(mine[1:], row_id, 1, 1).reshape(-1)
    own_index = jnp.concatenate([near, own_index])

    own_points, x_wide, f_wide = setup(own_index, x_train, frequencies, phases)
    points = lax.all_to_all(
        jnp.broadcast_to(own_points[None], (cols,) + own_points.shape), "col", 0, 0, tiled=True
    )
    gathered0 = from_x(dual.astype(BF16))

    group_index = mine.reshape(STEPS, group_rows)
    counts, known1, known2 = known_parts(group_index, targets, noise, dual, velocity)
    gathered1 = lax.all_gather(known1, "row", axis=0, tiled=True)
    gathered2 = lax.all_gather(known2, "row", axis=0, tiled=True)
    sorted_index = back_from(by_place[:2], x_id, 1)
    sorted_index = jnp.stack([sorted_index[0], back_from(sorted_index[1], z_id, 1)])
    sorted_index = sorted_index.transpose(0, 3, 1, 2, 4)
    sorted_index = jnp.where(core_id == 0, sorted_index, jnp.flip(sorted_index, 1)).reshape(2, group_rows)

    lane = lax.broadcasted_iota(jnp.int32, (128, 4), 0)
    back = lax.broadcasted_iota(jnp.int32, (128, 4), 1)
    path_of = ((x_id - lane // own_paths % 4) % 4 * 4 + (z_id - back) % 4) * 2 + (core_id ^ (lane // 32 % 2))
    path_of = path_of * own_paths + lane % own_paths
    here = lax.broadcasted_iota(jnp.int32, (paths // 4, paths), 1) == path_of[: paths // 4, :1]
    here = here.astype(BF16)
    window_part = window_prior(f_wide.T, path_weights, x_window, factor)
    points, window_part, path_of, here, sorted_index = after(points, window_part, path_of, here, sorted_index)
    prior_window = lax.psum_scatter(window_part, "col", scatter_dimension=0, tiled=True)
    gathered0 = jnp.concatenate(with_other_core(gathered0), axis=0)

    blocks = first_block(points, x_wide, gathered0, f_wide, path_weights, here, factor)
    row_index = lax.dynamic_slice_in_dim(batch_index[1], row_id * batch_rows, batch_rows, 0) - col_id * train

    def add_up(blocks):
        return jnp.sum(blocks.astype(F32), axis=0)

    chooser = lax.broadcasted_iota(jnp.int32, (own_paths, paths), 1)
    chooser = chooser - own_paths * row_id == lax.broadcasted_iota(jnp.int32, (own_paths, paths), 0)
    chooser = chooser.astype(BF16)

    blocks = lax.all_to_all(blocks, "col", 0, 0, tiled=True)
    group_points = pick_cols(sorted_index, x_train)
    blocks, group_points = after(blocks, group_points)
    terms0 = from_z(add_up(blocks).astype(BF16))
    between10 = pair_block(points, 4, group_points, 0, row_index[:, None], sorted_index[:1])
    *terms0, between10 = after(*terms0, between10)
    terms0 = from_x(merge(path_of, terms0))
    part1 = part_block(points, 4, x_wide, gathered1, f_wide, path_weights, factor)
    *terms0, part1 = after(*terms0, part1)
    terms0 = with_other_core(terms0)

    blocks = chain(part1, between10, terms0).reshape(cols, own_rows, paths)
    blocks = lax.all_to_all(blocks, "col", 0, 0, tiled=True)
    between21 = pair_block(points, 5, group_points, 1)
    blocks, between21 = after(blocks, between21)
    terms1 = from_z(add_up(blocks).astype(BF16))
    part2 = part_block(points, 5, x_wide, gathered2, f_wide, path_weights, factor)
    *terms1, part2 = after(*terms1, part2)
    terms1 = from_x(jnp.concatenate(terms1, axis=0))
    part2 = fold(part2, points, 5, group_points, 0, terms0)
    *terms1, part2 = after(*terms1, part2)
    terms1 = with_other_core(terms1)

    blocks = last(part2, between21, terms1).reshape(rows * cols, own_paths, own_rows)
    blocks = lax.all_to_all(blocks, ("row", "col"), 0, 0, tiled=True)
    z0 = place(sorted_index[0], chooser, terms0, train)
    z1 = place(sorted_index[1], chooser, terms1, train)
    blocks, z0, z1 = after(blocks, z0, z1)
    blocks = blocks.reshape(rows, cols, own_paths, own_rows)
    dual, velocity = finish(
        group_index[2], blocks, z0, z1, counts, targets, noise, dual, velocity
    )
    return (dual.T, velocity.T, prior_window)


def solution(mesh):
    placed = (
        P(None, "col"),
        P("col"),
        P("col", "row"),
        P("col", "row"),
        P("col", "row"),
        P(None, "col"),
        P("col"),
        P("col", None),
        P(None, "row"),
        P(),
    )
    return jax.shard_map(
        shards,
        mesh=mesh,
        in_specs=placed,
        out_specs=(P("col", "row"), P("col", "row"), P("col", "row")),
        check_vma=False,
    )
```

```python
import jax
import jax.numpy as jnp
import numpy as np
from jax import lax
from jax.experimental import pallas as pl
from jax.experimental.pallas import tpu as pltpu
from jax.sharding import PartitionSpec as P

STEPS = 3
NOISE_VAR = 0.25
MOMENTUM = 0.9
STEP_SIZE = 0.5
LENGTH = 1.15
F32 = jnp.float32
BF16 = jnp.bfloat16
SCALE = float(np.sqrt(3.0) / LENGTH)
LOG2_E = float(1.0 / np.log(2.0))
NN = (((1,), (0,)), ((), ()))
NT = (((1,), (1,)), ((), ()))


def cosine_fit(factor):
    top = 0.2501
    nodes = (np.cos((2 * np.arange(200) + 1) * np.pi / 400) + 1) * top / 2
    wanted = np.sqrt(2.0 * factor) * np.cos(np.pi * np.sqrt(nodes))
    fit = np.polynomial.chebyshev.Chebyshev.fit(nodes, wanted, 5, domain=[0, top])
    return [float(v) for v in fit.convert(kind=np.polynomial.Polynomial).coef]


def dot(a, b, dims=NN):
    return lax.dot_general(a, b, dims, preferred_element_type=F32)


def scaled_cos(half_arg, factor):
    coefs = cosine_fit(factor)
    turns = half_arg * (1.0 / np.pi)
    f = turns - jnp.round(turns)
    z = f * f
    c = z * coefs[-1] + coefs[-2]
    for coef in coefs[-3::-1]:
        c = c * z + coef
    return c * c - factor


def matern_of(dist_sq):
    dist_sq = jnp.maximum(dist_sq, 1e-30)
    dist = dist_sq * lax.rsqrt(dist_sq)
    return (dist * SCALE + 1.0) * jnp.exp2(dist * (-SCALE * LOG2_E))


def three_parts(x):
    high = x.astype(BF16).astype(F32)
    middle = (x - high).astype(BF16).astype(F32)
    return high, middle, x - high - middle


def wide_columns(body, first, second):
    cols = body.shape[1]
    row = lax.broadcasted_iota(jnp.int32, (16, cols), 0)
    high, middle, low = three_parts(second)
    extra = jnp.where(row < 3, first, 0.0)
    extra = jnp.where(row == 3, high, extra)
    extra = jnp.where(row == 4, middle, extra)
    extra = jnp.where(row == 5, low, extra)
    return jnp.concatenate(
        [body.astype(BF16), extra.astype(BF16), jnp.zeros((48, cols), BF16)], axis=0
    )


def distance_columns(b):
    return wide_columns(b * -2.0, 1.0, jnp.sum(b * b, axis=0, keepdims=True))


def setup_kernel(i_ref, x_ref, f_ref, ph_ref, p_ref, xo_ref, fo_ref):
    index = i_ref[...]
    high, low = index & 255, index >> 8
    onehot = (lax.broadcasted_iota(jnp.int32, (index.shape[0], 256), 1) == high).astype(F32).astype(BF16)
    total = jnp.zeros((index.shape[0], x_ref.shape[0]), F32)
    for part in range(x_ref.shape[1] // 256):
        found = dot(onehot, x_ref[:, part * 256 : (part + 1) * 256], NT)
        total = total + jnp.where(low == part, found, 0.0)
    high, middle, low = three_parts(jnp.sum(total * total, axis=1, keepdims=True))
    lane = lax.broadcasted_iota(jnp.int32, total.shape, 1)
    extra = jnp.where(lane < 6, 1.0, 0.0)
    extra = jnp.where(lane == 0, high, extra)
    extra = jnp.where(lane == 1, middle, extra)
    extra = jnp.where(lane == 2, low, extra)
    for copy in range(p_ref.shape[0]):
        p_ref[copy, :, :64] = total.astype(BF16)
        p_ref[copy, :, 64:] = extra.astype(BF16)
    for at in range(0, x_ref.shape[1], 512):
        xo_ref[:, at : at + 512] = distance_columns(x_ref[:, at : at + 512].astype(F32))
    fo_ref[...] = wide_columns(f_ref[...].astype(F32) * 0.5, 0.0, ph_ref[...] * 0.5)


def setup(index, x_train, frequencies, phases, copies):
    return pl.pallas_call(
        setup_kernel,
        out_shape=(
            jax.ShapeDtypeStruct((copies, index.shape[0], 128), BF16),
            jax.ShapeDtypeStruct((128, x_train.shape[1]), BF16),
            jax.ShapeDtypeStruct((128, frequencies.shape[1]), BF16),
        ),
        compiler_params=pltpu.CompilerParams(vmem_limit_bytes=24 << 20),
        cost_estimate=pl.CostEstimate(flops=1 << 22, bytes_accessed=2 << 20, transcendentals=0),
        name="setup",
    )(index[:, None], x_train, frequencies, phases[None, :])


def pick_cols_kernel(i_ref, x_ref, o_ref):
    index = i_ref[0]
    high, low = index & 255, index >> 8
    onehot = (lax.broadcasted_iota(jnp.int32, (256, index.shape[1]), 0) == high).astype(F32).astype(BF16)
    parts = x_ref.shape[1] // 256
    stacked = jnp.concatenate([x_ref[:, k * 256 : (k + 1) * 256] for k in range(parts)], axis=0)
    found = dot(stacked, onehot)
    total = jnp.zeros((x_ref.shape[0], index.shape[1]), F32)
    for k in range(parts):
        total = total + jnp.where(low == k, found[k * 64 : (k + 1) * 64], 0.0)
    o_ref[0] = distance_columns(total)


def pick_cols(index, x_train, block=512):
    steps, count = index.shape
    return pl.pallas_call(
        pick_cols_kernel,
        grid=(steps, count // block),
        in_specs=[
            pl.BlockSpec((1, 1, block), lambda t, i: (t, 0, i)),
            pl.BlockSpec(x_train.shape, lambda t, i: (0, 0)),
        ],
        out_specs=pl.BlockSpec((1, 128, block), lambda t, i: (t, 0, i)),
        out_shape=jax.ShapeDtypeStruct((steps, 128, count), BF16),
        compiler_params=pltpu.CompilerParams(vmem_limit_bytes=24 << 20),
        cost_estimate=pl.CostEstimate(
            flops=60 * steps * count * 256, bytes_accessed=1 << 20, transcendentals=0
        ),
        name="pick_cols",
    )(index[:, None, :], x_train)


def pair_kernel(p_ref, b_ref, *refs):
    p = p_ref[...].reshape(-1, 128)
    for at in range(0, b_ref.shape[2], 256):
        value = matern_of(dot(p, b_ref[0, :, at : at + 256]))
        if len(refs) == 3:
            same = refs[0][...] == refs[1][:, at : at + 256]
            value = value + jnp.where(same, NOISE_VAR, 0.0)
        refs[-1][:, at : at + 256] = value.astype(BF16)


def pair_block(points, place, others, other, point_ids=None, other_ids=None, block=1024):
    groups, rows, cols = points.shape[0], points.shape[0] * 64, others.shape[2]
    specs = [
        pl.BlockSpec((groups, 64, 128), lambda i: (0, place, 0)),
        pl.BlockSpec((1, 128, block), lambda i: (other, 0, i)),
    ]
    operands = [points, others]
    if point_ids is not None:
        specs += [pl.BlockSpec((rows, 1), lambda i: (0, 0)), pl.BlockSpec((1, block), lambda i: (0, i))]
        operands += [point_ids, other_ids]
    return pl.pallas_call(
        pair_kernel,
        grid=(cols // block,),
        in_specs=specs,
        out_specs=pl.BlockSpec((rows, block), lambda i: (0, i)),
        out_shape=jax.ShapeDtypeStruct((rows, cols), BF16),
        compiler_params=pltpu.CompilerParams(vmem_limit_bytes=24 << 20),
        cost_estimate=pl.CostEstimate(
            flops=12 * rows * cols, bytes_accessed=2 * rows * cols, transcendentals=2 * rows * cols
        ),
        name="pair_block",
    )(*operands)


def part_sums(p, x_ref, a_ref, f_ref, w, factor):
    total = dot(scaled_cos(dot(p, f_ref[...]), factor).astype(BF16), w)
    for at in range(0, x_ref.shape[1], 256):
        values = matern_of(dot(p, x_ref[:, at : at + 256])).astype(BF16)
        total = total + dot(values, a_ref[:, at : at + 256], NT)
    return total


def part_kernel(p_ref, x_ref, a_ref, f_ref, w_ref, o_ref, *, factor):
    total = part_sums(p_ref[...].reshape(-1, 128), x_ref, a_ref, f_ref, w_ref[...], factor)
    first = pl.program_id(0) == 0

    @pl.when(first)
    def _():
        o_ref[...] = total

    @pl.when(jnp.logical_not(first))
    def _():
        o_ref[...] += total


def part_block(points, place, x_wide, dual, f_wide, weights, factor, blocks=2):
    groups, rows, train = points.shape[0], points.shape[0] * 64, x_wide.shape[1]
    feats, paths = weights.shape
    return pl.pallas_call(
        lambda *refs: part_kernel(*refs, factor=factor),
        grid=(blocks,),
        in_specs=[
            pl.BlockSpec((groups, 64, 128), lambda i: (0, place, 0)),
            pl.BlockSpec((128, train // blocks), lambda i: (0, i)),
            pl.BlockSpec((paths, train // blocks), lambda i: (0, i)),
            pl.BlockSpec((128, feats // blocks), lambda i: (0, i)),
            pl.BlockSpec((feats // blocks, paths), lambda i: (i, 0)),
        ],
        out_specs=pl.BlockSpec((rows, paths), lambda i: (0, 0)),
        out_shape=jax.ShapeDtypeStruct((rows, paths), F32),
        compiler_params=pltpu.CompilerParams(vmem_limit_bytes=28 << 20),
        cost_estimate=pl.CostEstimate(
            flops=12 * rows * train, bytes_accessed=4 << 20, transcendentals=2 * rows * train
        ),
        name="part_block",
    )(points, x_wide, dual, f_wide, weights)


def first_kernel(p_ref, x_ref, a_ref, f_ref, w_ref, c_ref, o_ref, sum_ref, *, factor):
    col, row = pl.program_id(0), pl.program_id(1)
    weights = dot(w_ref[...], c_ref[...], NT).astype(BF16)
    total = part_sums(p_ref[...].reshape(-1, 128), x_ref, a_ref, f_ref, weights, factor)
    rows = total.shape[0]
    at = pl.ds(pl.multiple_of(row * rows, rows), rows)

    @pl.when(col == 0)
    def _():
        sum_ref[at, :] = total

    @pl.when(col > 0)
    def _():
        sum_ref[at, :] += total

    @pl.when(col == pl.num_programs(0) - 1)
    def _():
        done = sum_ref[at, :].astype(BF16).reshape(rows // 256, 2, 128, 64)
        for group in range(rows // 256):
            o_ref[group, :, :64] = done[group, 0]
            o_ref[group, :, 64:] = done[group, 1]


def first_block(points, x_wide, dual, f_wide, weights, chooser, factor, blocks=2):
    groups, train = points.shape[0], x_wide.shape[1]
    feats, paths = weights.shape
    some, chunk = dual.shape[0], 4
    return pl.pallas_call(
        lambda *refs: first_kernel(*refs, factor=factor),
        grid=(blocks, groups // chunk),
        in_specs=[
            pl.BlockSpec((chunk, 256, 128), lambda i, j: (j, 0, 0)),
            pl.BlockSpec((128, train // blocks), lambda i, j: (0, i)),
            pl.BlockSpec((some, train // blocks), lambda i, j: (0, i)),
            pl.BlockSpec((128, feats // blocks), lambda i, j: (0, i)),
            pl.BlockSpec((feats // blocks, paths), lambda i, j: (i, 0)),
            pl.BlockSpec((some, paths), lambda i, j: (0, 0)),
        ],
        out_specs=pl.BlockSpec((chunk, 128, 128), lambda i, j: (j, 0, 0)),
        out_shape=jax.ShapeDtypeStruct((groups, 128, 128), BF16),
        scratch_shapes=[pltpu.VMEM((groups * 256, some), F32)],
        compiler_params=pltpu.CompilerParams(vmem_limit_bytes=28 << 20),
        cost_estimate=pl.CostEstimate(
            flops=12 * groups * 256 * train, bytes_accessed=4 << 20, transcendentals=2 * groups * 256 * train
        ),
        name="first_block",
    )(points, x_wide, dual, f_wide, weights, chooser)


def merge_kernel(to_ref, b0_ref, b1_ref, b2_ref, b3_ref, o_ref):
    lane = lax.broadcasted_iota(jnp.int32, (128, 256), 0)
    path = lax.broadcasted_iota(jnp.int32, (128, 256), 1)
    for half in range(2):
        total = jnp.zeros((128, 256), F32)
        for k, b_ref in enumerate((b0_ref, b1_ref, b2_ref, b3_ref)):
            found = (path == to_ref[:, k : k + 1]) & (lane >> 6 == half)
            total = total + dot(b_ref[...], jnp.where(found, 1.0, 0.0).astype(BF16))
        o_ref[half * 128 : (half + 1) * 128, :] = total.astype(BF16)


def merge(to, blocks):
    return pl.pallas_call(
        merge_kernel, out_shape=jax.ShapeDtypeStruct((256, 256), BF16), name="merge"
    )(to, *blocks)


def chain_kernel(part_ref, k_ref, *refs):
    total = part_ref[...]
    cols = refs[0].shape[0]
    for i, r_ref in enumerate(refs[:-1]):
        total = total - STEP_SIZE * dot(k_ref[:, i * cols : (i + 1) * cols], r_ref[...])
    refs[-1][...] = total.astype(BF16)


def chain(part, block, pieces):
    return pl.pallas_call(
        chain_kernel,
        out_shape=jax.ShapeDtypeStruct(part.shape, BF16),
        compiler_params=pltpu.CompilerParams(vmem_limit_bytes=16 << 20),
        cost_estimate=pl.CostEstimate(flops=1 << 29, bytes_accessed=4 << 20, transcendentals=0),
        name="chain",
    )(part, block, *pieces)


def last_kernel(part_ref, k_ref, *refs):
    total = part_ref[...]
    cols = refs[0].shape[0]
    for i, r_ref in enumerate(refs[:-1]):
        total = total - STEP_SIZE * dot(k_ref[:, i * cols : (i + 1) * cols], r_ref[...])
    turned = total.T
    o_ref = refs[-1]
    for c in range(o_ref.shape[1]):
        o_ref[:, c] = turned[:, c * 64 : (c + 1) * 64].reshape(o_ref.shape[0], 8, 64).astype(BF16)


def last(part, block, pieces):
    rows, paths = part.shape
    return pl.pallas_call(
        last_kernel,
        out_shape=jax.ShapeDtypeStruct((paths // 8, rows // 64, 8, 64), BF16),
        compiler_params=pltpu.CompilerParams(vmem_limit_bytes=16 << 20),
        cost_estimate=pl.CostEstimate(flops=1 << 29, bytes_accessed=4 << 20, transcendentals=0),
        name="last",
    )(part, block, *pieces)


def fold_kernel(part_ref, p_ref, b_ref, *refs):
    p = p_ref[...].reshape(-1, 128)
    total = part_ref[...]
    cols = refs[0].shape[0]
    for i, r_ref in enumerate(refs[:-1]):
        values = matern_of(dot(p, b_ref[0, :, i * cols : (i + 1) * cols])).astype(BF16)
        total = total - (STEP_SIZE * (1.0 + MOMENTUM)) * dot(values, r_ref[...])
    refs[-1][...] = total


def fold(part, points, place, others, other, pieces):
    whole = pl.BlockSpec(part.shape, lambda i: (0, 0))
    piece = pl.BlockSpec(pieces[0].shape, lambda i: (0, 0))
    return pl.pallas_call(
        fold_kernel,
        grid=(1,),
        in_specs=[
            whole,
            pl.BlockSpec((points.shape[0], 64, 128), lambda i: (0, place, 0)),
            pl.BlockSpec((1,) + others.shape[1:], lambda i: (other, 0, 0)),
        ]
        + [piece] * len(pieces),
        out_specs=whole,
        out_shape=jax.ShapeDtypeStruct(part.shape, F32),
        compiler_params=pltpu.CompilerParams(vmem_limit_bytes=24 << 20),
        cost_estimate=pl.CostEstimate(flops=1 << 29, bytes_accessed=4 << 20, transcendentals=1 << 21),
        name="fold",
    )(part, points, others, *pieces)


def window_kernel(f_ref, w_ref, x_ref, o_ref, *, factor):
    cols = x_ref.shape[1]
    row = lax.broadcasted_iota(jnp.int32, (16, cols), 0)
    ones = jnp.where((row >= 3) & (row < 6), 1.0, 0.0).astype(BF16)
    x = jnp.concatenate([x_ref[...], ones, jnp.zeros((48, cols), BF16)], axis=0)
    for at in range(0, cols, 256):
        phi = scaled_cos(dot(f_ref[...], x[:, at : at + 256]), factor).astype(BF16)
        o_ref[:, at : at + 256] = dot(w_ref[...], phi)


def window_prior(f_rows, weights, x_window, factor, block=1024):
    feats, paths, window = f_rows.shape[0], weights.shape[1], x_window.shape[1]
    return pl.pallas_call(
        lambda *refs: window_kernel(*refs, factor=factor),
        grid=(window // block,),
        in_specs=[
            pl.BlockSpec((feats, 128), lambda i: (0, 0)),
            pl.BlockSpec((paths, feats), lambda i: (0, 0)),
            pl.BlockSpec((x_window.shape[0], block), lambda i: (0, i)),
        ],
        out_specs=pl.BlockSpec((paths, block), lambda i: (0, i)),
        out_shape=jax.ShapeDtypeStruct((paths, window), F32),
        compiler_params=pltpu.CompilerParams(vmem_limit_bytes=24 << 20),
        cost_estimate=pl.CostEstimate(
            flops=24 * feats * window, bytes_accessed=4 * paths * window, transcendentals=feats * window
        ),
        name="window_prior",
    )(f_rows, weights.T, x_window)


def spread(index, rows, train):
    high, low = index >> 7, index & 127
    low_hot = (lax.broadcasted_iota(jnp.int32, (128, index.shape[1]), 0) == low).astype(F32).astype(BF16)
    tiles = [jnp.where(high == h, rows, 0.0) for h in range(train // 128)]
    return dot(jnp.concatenate(tiles, axis=0).astype(BF16), low_hot, NT)


def known_kernel(i_ref, t_ref, n_ref, a_ref, v_ref, cnt_ref, known_ref):
    train = a_ref.shape[1]
    ones = jnp.ones((8, i_ref.shape[1]), F32)
    for t in range(STEPS):
        tiles = spread(i_ref[t : t + 1, :], ones, train)
        for h in range(train // 128):
            cnt_ref[t, :, h * 128 : (h + 1) * 128] = tiles[h * 8 : (h + 1) * 8, :]
    dual, velocity = a_ref[...], v_ref[...]
    fixed = n_ref[...] - t_ref[...]
    for t in range(STEPS - 1):
        gradient = cnt_ref[t] * (NOISE_VAR * dual + fixed)
        velocity = MOMENTUM * velocity - STEP_SIZE * gradient
        dual = dual + velocity
        known_ref[t * 8 : (t + 1) * 8, :] = dual.astype(BF16)


def known_parts(index, targets, noise, dual, velocity):
    shape = dual.shape
    return pl.pallas_call(
        known_kernel,
        out_shape=(
            jax.ShapeDtypeStruct((STEPS,) + shape, F32),
            jax.ShapeDtypeStruct(((STEPS - 1) * shape[0], shape[1]), BF16),
        ),
        compiler_params=pltpu.CompilerParams(vmem_limit_bytes=32 << 20),
        cost_estimate=pl.CostEstimate(flops=1 << 23, bytes_accessed=1 << 20, transcendentals=0),
        name="known_parts",
    )(index, targets[None, :], noise, dual, velocity)


def place_kernel(i_ref, c_ref, *refs):
    o_ref = refs[-1]
    train = o_ref.shape[1]
    rows = jnp.concatenate([dot(c_ref[...], r_ref[...], NT) for r_ref in refs[:-1]], axis=1)
    tiles = spread(i_ref[...], rows, train)
    for h in range(train // 128):
        o_ref[:, h * 128 : (h + 1) * 128] = tiles[h * 8 : (h + 1) * 8, :]


def place(index, chooser, pieces, train):
    return pl.pallas_call(
        place_kernel,
        out_shape=jax.ShapeDtypeStruct((8, train), F32),
        compiler_params=pltpu.CompilerParams(vmem_limit_bytes=32 << 20),
        cost_estimate=pl.CostEstimate(flops=1 << 22, bytes_accessed=1 << 20, transcendentals=0),
        name="place",
    )(index[None, :], chooser, *pieces)


def finish_kernel(i_ref, r_ref, z0_ref, z1_ref, cnt_ref, t_ref, n_ref, a_ref, v_ref, ao_ref, vo_ref, rows_ref):
    train = a_ref.shape[1]
    for r in range(r_ref.shape[0]):
        rows_ref[:, r * 64 : (r + 1) * 64] = jnp.sum(r_ref[r].astype(F32), axis=0)
    rows = rows_ref[...]
    coarse = rows.astype(BF16).astype(F32)
    tiles = spread(i_ref[...], coarse, train) + spread(i_ref[...], rows - coarse, train)
    dual, velocity = a_ref[...], v_ref[...]
    fixed = n_ref[...] - t_ref[...]
    z0 = z0_ref[...]
    velocity = MOMENTUM * velocity - STEP_SIZE * (z0 + cnt_ref[0] * (NOISE_VAR * dual + fixed))
    dual = dual + velocity
    change = -STEP_SIZE * z0
    gradient = z1_ref[...] + cnt_ref[1] * (NOISE_VAR * (dual - change) + fixed)
    velocity = MOMENTUM * velocity - STEP_SIZE * gradient
    dual = dual + velocity
    base = cnt_ref[2] * (NOISE_VAR * dual + fixed)
    for h in range(train // 128):
        at = slice(h * 128, (h + 1) * 128)
        vo_ref[:, at] = MOMENTUM * velocity[:, at] - STEP_SIZE * (
            base[:, at] + tiles[h * 8 : (h + 1) * 8, :]
        )
    ao_ref[...] = dual + vo_ref[...]


def finish(index, rows, z0, z1, counts, targets, noise, dual, velocity):
    shape = jax.ShapeDtypeStruct(dual.shape, F32)
    return pl.pallas_call(
        finish_kernel,
        out_shape=(shape, shape),
        scratch_shapes=[pltpu.VMEM((8, rows.shape[0] * 64), F32)],
        compiler_params=pltpu.CompilerParams(vmem_limit_bytes=48 << 20),
        cost_estimate=pl.CostEstimate(flops=1 << 22, bytes_accessed=1 << 20, transcendentals=0),
        name="finish",
    )(index[None, :], rows, z0, z1, counts, targets[None, :], noise, dual, velocity)


def row_moves(dx, dz, dcore):
    return [
        ((x * 4 + z) * 2 + core, ((x + dx) % 4 * 4 + (z + dz) % 4) * 2 + (core ^ dcore))
        for x in range(4)
        for z in range(4)
        for core in range(2)
    ]


def from_x(block):
    return [block] + [lax.ppermute(block, "row", row_moves(d, 0, 0)) for d in (1, 2, 3)]


def from_z(block):
    return [block] + [lax.ppermute(block, "row", row_moves(0, d, 0)) for d in (1, 2, 3)]


def with_other_core(blocks):
    return blocks + [lax.ppermute(block, "row", row_moves(0, 0, 1)) for block in blocks]


def back_from(array, here, axis):
    turned = jnp.flip(array, axis)
    return lax.dynamic_slice_in_dim(jnp.concatenate([turned, turned], axis), 3 - here, 4, axis)


def after(*values):
    return lax.optimization_barrier(values)


def shards(
    x_train,
    targets,
    noise_draws,
    alpha_init,
    velocity_init,
    frequencies,
    phases,
    path_weights,
    x_window,
    batch_index,
):
    rows, cols = lax.axis_size("row"), lax.axis_size("col")
    row_id, col_id = lax.axis_index("row"), lax.axis_index("col")
    train = x_train.shape[1]
    batch_rows = batch_index.shape[1] // rows
    own_rows = batch_rows // cols
    group_rows = rows * own_rows
    paths = path_weights.shape[1]
    own_paths = paths // rows
    factor = (2.0 / (frequencies.shape[1] * cols)) ** 0.5
    dual, velocity, noise = alpha_init.T, velocity_init.T, noise_draws.T
    x_id, z_id, core_id = row_id // 8, row_id // 2 % 4, row_id % 2

    by_group = batch_index.reshape(STEPS, rows, cols, own_rows)
    mine = lax.dynamic_slice_in_dim(by_group, col_id, 1, 2)[:, :, 0] - col_id * train
    by_place = mine.reshape(STEPS, 4, 4, 2, own_rows)
    near = lax.dynamic_slice(by_place[0], (x_id, 0, core_id, 0), (1, 4, 1, own_rows)).reshape(-1)
    own_index = lax.dynamic_slice_in_dim(mine[1:], row_id, 1, 1).reshape(-1)
    own_index = jnp.concatenate([near, own_index])

    own_points, x_wide, f_wide = setup(own_index, x_train, frequencies, phases, cols)
    own_points, x_wide, dual, velocity, noise, mine = after(
        own_points, x_wide, dual, velocity, noise, mine
    )
    points = lax.all_to_all(own_points, "col", 0, 0, tiled=True)
    gathered0 = from_x(dual.astype(BF16))

    group_index = mine.reshape(STEPS, group_rows)
    counts, known = known_parts(group_index, targets, noise, dual, velocity)
    gathered = lax.all_gather(known, "row", axis=0, tiled=True).reshape(rows, STEPS - 1, own_paths, train)
    gathered1, gathered2 = (gathered[:, t].reshape(paths, train) for t in range(STEPS - 1))
    sorted_index = back_from(by_place[:2], x_id, 1)
    sorted_index = jnp.stack([sorted_index[0], back_from(sorted_index[1], z_id, 1)])
    sorted_index = sorted_index.transpose(0, 3, 1, 2, 4)
    sorted_index = jnp.where(core_id == 0, sorted_index, jnp.flip(sorted_index, 1)).reshape(2, group_rows)

    lane = lax.broadcasted_iota(jnp.int32, (128, 4), 0)
    back = lax.broadcasted_iota(jnp.int32, (128, 4), 1)
    path_of = ((x_id - lane // own_paths % 4) % 4 * 4 + (z_id - back) % 4) * 2 + (core_id ^ (lane // 32 % 2))
    path_of = path_of * own_paths + lane % own_paths
    here = lax.broadcasted_iota(jnp.int32, (paths // 4, paths), 1) == path_of[: paths // 4, :1]
    here = here.astype(BF16)
    window_part = window_prior(f_wide.T, path_weights, x_window, factor)
    points, window_part, path_of, here, sorted_index = after(points, window_part, path_of, here, sorted_index)
    prior_window = lax.psum_scatter(window_part, "col", scatter_dimension=0, tiled=True)
    gathered0 = jnp.concatenate(with_other_core(gathered0), axis=0)

    blocks = first_block(points, x_wide, gathered0, f_wide, path_weights, here, factor)
    row_index = lax.dynamic_slice_in_dim(batch_index[1], row_id * batch_rows, batch_rows, 0) - col_id * train

    def add_up(blocks):
        return jnp.sum(blocks.astype(F32), axis=0)

    chooser = lax.broadcasted_iota(jnp.int32, (own_paths, paths), 1)
    chooser = chooser - own_paths * row_id == lax.broadcasted_iota(jnp.int32, (own_paths, paths), 0)
    chooser = chooser.astype(BF16)

    blocks = lax.all_to_all(blocks, "col", 0, 0, tiled=True)
    group_points = pick_cols(sorted_index, x_train)
    blocks, group_points = after(blocks, group_points)
    terms0 = from_z(add_up(blocks).astype(BF16))
    between10 = pair_block(points, 4, group_points, 0, row_index[:, None], sorted_index[:1])
    *terms0, between10 = after(*terms0, between10)
    terms0 = from_x(merge(path_of, terms0))
    part1 = part_block(points, 4, x_wide, gathered1, f_wide, path_weights, factor)
    *terms0, part1 = after(*terms0, part1)
    terms0 = with_other_core(terms0)

    blocks = chain(part1, between10, terms0).reshape(cols, own_rows, paths)
    blocks = lax.all_to_all(blocks, "col", 0, 0, tiled=True)
    between21 = pair_block(points, 5, group_points, 1)
    blocks, between21 = after(blocks, between21)
    terms1 = from_z(add_up(blocks).astype(BF16))
    part2 = part_block(points, 5, x_wide, gathered2, f_wide, path_weights, factor)
    *terms1, part2 = after(*terms1, part2)
    terms1 = from_x(jnp.concatenate(terms1, axis=0))
    part2 = fold(part2, points, 5, group_points, 0, terms0)
    *terms1, part2 = after(*terms1, part2)
    terms1 = with_other_core(terms1)

    blocks = last(part2, between21, terms1).reshape(rows * cols, own_paths, own_rows)
    blocks = lax.all_to_all(blocks, ("row", "col"), 0, 0, tiled=True)
    z0 = place(sorted_index[0], chooser, terms0, train)
    z1 = place(sorted_index[1], chooser, terms1, train)
    blocks, z0, z1 = after(blocks, z0, z1)
    blocks = blocks.reshape(rows, cols, own_paths, own_rows)
    dual, velocity = finish(
        group_index[2], blocks, z0, z1, counts, targets, noise, dual, velocity
    )
    return (dual.T, velocity.T, prior_window)


def solution(mesh):
    placed = (
        P(None, "col"),
        P("col"),
        P("col", "row"),
        P("col", "row"),
        P("col", "row"),
        P(None, "col"),
        P("col"),
        P("col", None),
        P(None, "row"),
        P(),
    )
    return jax.shard_map(
        shards,
        mesh=mesh,
        in_specs=placed,
        out_specs=(P("col", "row"), P("col", "row"), P("col", "row")),
        check_vma=False,
    )
```

```python
import jax
import jax.numpy as jnp
import numpy as np
from jax import lax
from jax.experimental import pallas as pl
from jax.experimental.pallas import tpu as pltpu
from jax.sharding import PartitionSpec as P

STEPS = 3
NOISE_VAR = 0.25
MOMENTUM = 0.9
STEP_SIZE = 0.5
LENGTH = 1.15
F32 = jnp.float32
BF16 = jnp.bfloat16
SCALE = float(np.sqrt(3.0) / LENGTH)
LOG2_E = float(1.0 / np.log(2.0))
NN = (((1,), (0,)), ((), ()))
NT = (((1,), (1,)), ((), ()))


def cosine_fit(factor):
    top = 0.2501
    nodes = (np.cos((2 * np.arange(200) + 1) * np.pi / 400) + 1) * top / 2
    wanted = np.sqrt(2.0 * factor) * np.cos(np.pi * np.sqrt(nodes))
    fit = np.polynomial.chebyshev.Chebyshev.fit(nodes, wanted, 5, domain=[0, top])
    return [float(v) for v in fit.convert(kind=np.polynomial.Polynomial).coef]


def dot(a, b, dims=NN):
    return lax.dot_general(a, b, dims, preferred_element_type=F32)


def scaled_cos(half_arg, factor):
    coefs = cosine_fit(factor)
    turns = half_arg * (1.0 / np.pi)
    f = turns - jnp.round(turns)
    z = f * f
    c = z * coefs[-1] + coefs[-2]
    for coef in coefs[-3::-1]:
        c = c * z + coef
    return c * c - factor


def matern_of(dist_sq):
    dist_sq = jnp.maximum(dist_sq, 1e-30)
    dist = dist_sq * lax.rsqrt(dist_sq)
    return (dist * SCALE + 1.0) * jnp.exp2(dist * (-SCALE * LOG2_E))


def three_parts(x):
    high = x.astype(BF16).astype(F32)
    middle = (x - high).astype(BF16).astype(F32)
    return high, middle, x - high - middle


def wide_columns(body, first, second):
    cols = body.shape[1]
    row = lax.broadcasted_iota(jnp.int32, (16, cols), 0)
    high, middle, low = three_parts(second)
    extra = jnp.where(row < 3, first, 0.0)
    extra = jnp.where(row == 3, high, extra)
    extra = jnp.where(row == 4, middle, extra)
    extra = jnp.where(row == 5, low, extra)
    return jnp.concatenate(
        [body.astype(BF16), extra.astype(BF16), jnp.zeros((48, cols), BF16)], axis=0
    )


def distance_columns(b):
    return wide_columns(b * -2.0, 1.0, jnp.sum(b * b, axis=0, keepdims=True))


def setup_kernel(i_ref, x_ref, f_ref, ph_ref, p_ref, xo_ref, fo_ref):
    index = i_ref[...]
    high, low = index & 255, index >> 8
    onehot = (lax.broadcasted_iota(jnp.int32, (index.shape[0], 256), 1) == high).astype(F32).astype(BF16)
    total = jnp.zeros((index.shape[0], x_ref.shape[0]), F32)
    for part in range(x_ref.shape[1] // 256):
        found = dot(onehot, x_ref[:, part * 256 : (part + 1) * 256], NT)
        total = total + jnp.where(low == part, found, 0.0)
    high, middle, low = three_parts(jnp.sum(total * total, axis=1, keepdims=True))
    lane = lax.broadcasted_iota(jnp.int32, total.shape, 1)
    extra = jnp.where(lane < 6, 1.0, 0.0)
    extra = jnp.where(lane == 0, high, extra)
    extra = jnp.where(lane == 1, middle, extra)
    extra = jnp.where(lane == 2, low, extra)
    for copy in range(p_ref.shape[0]):
        p_ref[copy, :, :64] = total.astype(BF16)
        p_ref[copy, :, 64:] = extra.astype(BF16)
    for at in range(0, x_ref.shape[1], 512):
        xo_ref[:, at : at + 512] = distance_columns(x_ref[:, at : at + 512].astype(F32))
    fo_ref[...] = wide_columns(f_ref[...].astype(F32) * 0.5, 0.0, ph_ref[...] * 0.5)


def setup(index, x_train, frequencies, phases, copies):
    return pl.pallas_call(
        setup_kernel,
        out_shape=(
            jax.ShapeDtypeStruct((copies, index.shape[0], 128), BF16),
            jax.ShapeDtypeStruct((128, x_train.shape[1]), BF16),
            jax.ShapeDtypeStruct((128, frequencies.shape[1]), BF16),
        ),
        compiler_params=pltpu.CompilerParams(vmem_limit_bytes=24 << 20),
        cost_estimate=pl.CostEstimate(flops=1 << 22, bytes_accessed=2 << 20, transcendentals=0),
        name="setup",
    )(index[:, None], x_train, frequencies, phases[None, :])


def pick_cols_kernel(i_ref, x_ref, o_ref):
    index = i_ref[0]
    high, low = index & 255, index >> 8
    onehot = (lax.broadcasted_iota(jnp.int32, (256, index.shape[1]), 0) == high).astype(F32).astype(BF16)
    parts = x_ref.shape[1] // 256
    stacked = jnp.concatenate([x_ref[:, k * 256 : (k + 1) * 256] for k in range(parts)], axis=0)
    found = dot(stacked, onehot)
    total = jnp.zeros((x_ref.shape[0], index.shape[1]), F32)
    for k in range(parts):
        total = total + jnp.where(low == k, found[k * 64 : (k + 1) * 64], 0.0)
    o_ref[0] = distance_columns(total)


def pick_cols(index, x_train, block=512):
    steps, count = index.shape
    return pl.pallas_call(
        pick_cols_kernel,
        grid=(steps, count // block),
        in_specs=[
            pl.BlockSpec((1, 1, block), lambda t, i: (t, 0, i)),
            pl.BlockSpec(x_train.shape, lambda t, i: (0, 0)),
        ],
        out_specs=pl.BlockSpec((1, 128, block), lambda t, i: (t, 0, i)),
        out_shape=jax.ShapeDtypeStruct((steps, 128, count), BF16),
        compiler_params=pltpu.CompilerParams(vmem_limit_bytes=24 << 20),
        cost_estimate=pl.CostEstimate(
            flops=60 * steps * count * 256, bytes_accessed=1 << 20, transcendentals=0
        ),
        name="pick_cols",
    )(index[:, None, :], x_train)


def pair_kernel(p_ref, b_ref, *refs):
    p = p_ref[...].reshape(-1, 128)
    for at in range(0, b_ref.shape[2], 256):
        value = matern_of(dot(p, b_ref[0, :, at : at + 256]))
        if len(refs) == 3:
            same = refs[0][...] == refs[1][:, at : at + 256]
            value = value + jnp.where(same, NOISE_VAR, 0.0)
        refs[-1][:, at : at + 256] = value.astype(BF16)


def pair_block(points, place, others, other, point_ids=None, other_ids=None, block=1024):
    groups, rows, cols = points.shape[0], points.shape[0] * 64, others.shape[2]
    specs = [
        pl.BlockSpec((groups, 64, 128), lambda i: (0, place, 0)),
        pl.BlockSpec((1, 128, block), lambda i: (other, 0, i)),
    ]
    operands = [points, others]
    if point_ids is not None:
        specs += [pl.BlockSpec((rows, 1), lambda i: (0, 0)), pl.BlockSpec((1, block), lambda i: (0, i))]
        operands += [point_ids, other_ids]
    return pl.pallas_call(
        pair_kernel,
        grid=(cols // block,),
        in_specs=specs,
        out_specs=pl.BlockSpec((rows, block), lambda i: (0, i)),
        out_shape=jax.ShapeDtypeStruct((rows, cols), BF16),
        compiler_params=pltpu.CompilerParams(vmem_limit_bytes=24 << 20),
        cost_estimate=pl.CostEstimate(
            flops=12 * rows * cols, bytes_accessed=2 * rows * cols, transcendentals=2 * rows * cols
        ),
        name="pair_block",
    )(*operands)


def part_sums(p, x_ref, a_ref, f_ref, w, factor):
    total = dot(scaled_cos(dot(p, f_ref[...]), factor).astype(BF16), w)
    for at in range(0, x_ref.shape[1], 256):
        values = matern_of(dot(p, x_ref[:, at : at + 256])).astype(BF16)
        total = total + dot(values, a_ref[:, at : at + 256], NT)
    return total


def part_kernel(p_ref, x_ref, a_ref, f_ref, w_ref, o_ref, *, factor):
    total = part_sums(p_ref[...].reshape(-1, 128), x_ref, a_ref, f_ref, w_ref[...], factor)
    first = pl.program_id(0) == 0

    @pl.when(first)
    def _():
        o_ref[...] = total

    @pl.when(jnp.logical_not(first))
    def _():
        o_ref[...] += total


def part_block(points, place, x_wide, dual, f_wide, weights, factor, blocks=2):
    groups, rows, train = points.shape[0], points.shape[0] * 64, x_wide.shape[1]
    feats, paths = weights.shape
    return pl.pallas_call(
        lambda *refs: part_kernel(*refs, factor=factor),
        grid=(blocks,),
        in_specs=[
            pl.BlockSpec((groups, 64, 128), lambda i: (0, place, 0)),
            pl.BlockSpec((128, train // blocks), lambda i: (0, i)),
            pl.BlockSpec((paths, train // blocks), lambda i: (0, i)),
            pl.BlockSpec((128, feats // blocks), lambda i: (0, i)),
            pl.BlockSpec((feats // blocks, paths), lambda i: (i, 0)),
        ],
        out_specs=pl.BlockSpec((rows, paths), lambda i: (0, 0)),
        out_shape=jax.ShapeDtypeStruct((rows, paths), F32),
        compiler_params=pltpu.CompilerParams(vmem_limit_bytes=28 << 20),
        cost_estimate=pl.CostEstimate(
            flops=12 * rows * train, bytes_accessed=4 << 20, transcendentals=2 * rows * train
        ),
        name="part_block",
    )(points, x_wide, dual, f_wide, weights)


def first_kernel(p_ref, x_ref, a_ref, f_ref, w_ref, c_ref, o_ref, sum_ref, *, factor):
    col, row = pl.program_id(0), pl.program_id(1)
    weights = dot(w_ref[...], c_ref[...], NT).astype(BF16)
    total = part_sums(p_ref[...].reshape(-1, 128), x_ref, a_ref, f_ref, weights, factor)
    rows = total.shape[0]
    at = pl.ds(pl.multiple_of(row * rows, rows), rows)

    @pl.when(col == 0)
    def _():
        sum_ref[at, :] = total

    @pl.when(col > 0)
    def _():
        sum_ref[at, :] += total

    @pl.when(col == pl.num_programs(0) - 1)
    def _():
        done = sum_ref[at, :].astype(BF16).reshape(rows // 256, 2, 128, 64)
        for group in range(rows // 256):
            o_ref[group, :, :64] = done[group, 0]
            o_ref[group, :, 64:] = done[group, 1]


def first_block(points, x_wide, dual, f_wide, weights, chooser, factor, blocks=2):
    groups, train = points.shape[0], x_wide.shape[1]
    feats, paths = weights.shape
    some, chunk = dual.shape[0], 4
    return pl.pallas_call(
        lambda *refs: first_kernel(*refs, factor=factor),
        grid=(blocks, groups // chunk),
        in_specs=[
            pl.BlockSpec((chunk, 256, 128), lambda i, j: (j, 0, 0)),
            pl.BlockSpec((128, train // blocks), lambda i, j: (0, i)),
            pl.BlockSpec((some, train // blocks), lambda i, j: (0, i)),
            pl.BlockSpec((128, feats // blocks), lambda i, j: (0, i)),
            pl.BlockSpec((feats // blocks, paths), lambda i, j: (i, 0)),
            pl.BlockSpec((some, paths), lambda i, j: (0, 0)),
        ],
        out_specs=pl.BlockSpec((chunk, 128, 128), lambda i, j: (j, 0, 0)),
        out_shape=jax.ShapeDtypeStruct((groups, 128, 128), BF16),
        scratch_shapes=[pltpu.VMEM((groups * 256, some), F32)],
        compiler_params=pltpu.CompilerParams(vmem_limit_bytes=28 << 20),
        cost_estimate=pl.CostEstimate(
            flops=12 * groups * 256 * train, bytes_accessed=4 << 20, transcendentals=2 * groups * 256 * train
        ),
        name="first_block",
    )(points, x_wide, dual, f_wide, weights, chooser)


def merge_kernel(to_ref, b0_ref, b1_ref, b2_ref, b3_ref, o_ref):
    lane = lax.broadcasted_iota(jnp.int32, (128, 256), 0)
    path = lax.broadcasted_iota(jnp.int32, (128, 256), 1)
    for half in range(2):
        total = jnp.zeros((128, 256), F32)
        for k, b_ref in enumerate((b0_ref, b1_ref, b2_ref, b3_ref)):
            found = (path == to_ref[:, k : k + 1]) & (lane >> 6 == half)
            total = total + dot(b_ref[...], jnp.where(found, 1.0, 0.0).astype(BF16))
        o_ref[half * 128 : (half + 1) * 128, :] = total.astype(BF16)


def merge(to, blocks):
    return pl.pallas_call(
        merge_kernel, out_shape=jax.ShapeDtypeStruct((256, 256), BF16), name="merge"
    )(to, *blocks)


def chain_kernel(part_ref, k_ref, *refs):
    total = part_ref[...]
    cols = refs[0].shape[0]
    for i, r_ref in enumerate(refs[:-1]):
        total = total - STEP_SIZE * dot(k_ref[:, i * cols : (i + 1) * cols], r_ref[...])
    refs[-1][...] = total.astype(BF16)


def chain(part, block, pieces):
    return pl.pallas_call(
        chain_kernel,
        out_shape=jax.ShapeDtypeStruct(part.shape, BF16),
        compiler_params=pltpu.CompilerParams(vmem_limit_bytes=16 << 20),
        cost_estimate=pl.CostEstimate(flops=1 << 29, bytes_accessed=4 << 20, transcendentals=0),
        name="chain",
    )(part, block, *pieces)


def last_kernel(part_ref, k_ref, *refs):
    total = part_ref[...]
    cols = refs[0].shape[0]
    for i, r_ref in enumerate(refs[:-1]):
        total = total - STEP_SIZE * dot(k_ref[:, i * cols : (i + 1) * cols], r_ref[...])
    turned = total.T
    o_ref = refs[-1]
    for c in range(o_ref.shape[1]):
        block = turned[:, c * 64 : (c + 1) * 64].reshape(o_ref.shape[0], 8, 64)
        o_ref[:, c, :, :64] = block[:, :4].astype(BF16)
        o_ref[:, c, :, 64:] = block[:, 4:].astype(BF16)


def last(part, block, pieces):
    rows, paths = part.shape
    return pl.pallas_call(
        last_kernel,
        out_shape=jax.ShapeDtypeStruct((paths // 8, rows // 64, 4, 128), BF16),
        compiler_params=pltpu.CompilerParams(vmem_limit_bytes=16 << 20),
        cost_estimate=pl.CostEstimate(flops=1 << 29, bytes_accessed=4 << 20, transcendentals=0),
        name="last",
    )(part, block, *pieces)


def fold_kernel(part_ref, p_ref, b_ref, *refs):
    p = p_ref[...].reshape(-1, 128)
    total = part_ref[...]
    cols = refs[0].shape[0]
    for i, r_ref in enumerate(refs[:-1]):
        values = matern_of(dot(p, b_ref[0, :, i * cols : (i + 1) * cols])).astype(BF16)
        total = total - (STEP_SIZE * (1.0 + MOMENTUM)) * dot(values, r_ref[...])
    refs[-1][...] = total


def fold(part, points, place, others, other, pieces):
    whole = pl.BlockSpec(part.shape, lambda i: (0, 0))
    piece = pl.BlockSpec(pieces[0].shape, lambda i: (0, 0))
    return pl.pallas_call(
        fold_kernel,
        grid=(1,),
        in_specs=[
            whole,
            pl.BlockSpec((points.shape[0], 64, 128), lambda i: (0, place, 0)),
            pl.BlockSpec((1,) + others.shape[1:], lambda i: (other, 0, 0)),
        ]
        + [piece] * len(pieces),
        out_specs=whole,
        out_shape=jax.ShapeDtypeStruct(part.shape, F32),
        compiler_params=pltpu.CompilerParams(vmem_limit_bytes=24 << 20),
        cost_estimate=pl.CostEstimate(flops=1 << 29, bytes_accessed=4 << 20, transcendentals=1 << 21),
        name="fold",
    )(part, points, others, *pieces)


def window_kernel(f_ref, w_ref, x_ref, o_ref, *, factor):
    cols = x_ref.shape[1]
    row = lax.broadcasted_iota(jnp.int32, (16, cols), 0)
    ones = jnp.where((row >= 3) & (row < 6), 1.0, 0.0).astype(BF16)
    x = jnp.concatenate([x_ref[...], ones, jnp.zeros((48, cols), BF16)], axis=0)
    for at in range(0, cols, 256):
        phi = scaled_cos(dot(f_ref[...], x[:, at : at + 256]), factor).astype(BF16)
        o_ref[:, at : at + 256] = dot(w_ref[...], phi)


def window_prior(f_rows, weights, x_window, factor, block=1024):
    feats, paths, window = f_rows.shape[0], weights.shape[1], x_window.shape[1]
    return pl.pallas_call(
        lambda *refs: window_kernel(*refs, factor=factor),
        grid=(window // block,),
        in_specs=[
            pl.BlockSpec((feats, 128), lambda i: (0, 0)),
            pl.BlockSpec((paths, feats), lambda i: (0, 0)),
            pl.BlockSpec((x_window.shape[0], block), lambda i: (0, i)),
        ],
        out_specs=pl.BlockSpec((paths, block), lambda i: (0, i)),
        out_shape=jax.ShapeDtypeStruct((paths, window), F32),
        compiler_params=pltpu.CompilerParams(vmem_limit_bytes=24 << 20),
        cost_estimate=pl.CostEstimate(
            flops=24 * feats * window, bytes_accessed=4 * paths * window, transcendentals=feats * window
        ),
        name="window_prior",
    )(f_rows, weights.T, x_window)


def spread(index, rows, train):
    high, low = index >> 7, index & 127
    low_hot = (lax.broadcasted_iota(jnp.int32, (128, index.shape[1]), 0) == low).astype(F32).astype(BF16)
    tiles = [jnp.where(high == h, rows, 0.0) for h in range(train // 128)]
    return dot(jnp.concatenate(tiles, axis=0).astype(BF16), low_hot, NT)


def known_kernel(i_ref, t_ref, n_ref, a_ref, v_ref, cnt_ref, known_ref):
    train = a_ref.shape[1]
    ones = jnp.ones((8, i_ref.shape[1]), F32)
    for t in range(STEPS):
        tiles = spread(i_ref[t : t + 1, :], ones, train)
        for h in range(train // 128):
            cnt_ref[t, :, h * 128 : (h + 1) * 128] = tiles[h * 8 : (h + 1) * 8, :]
    dual, velocity = a_ref[...], v_ref[...]
    fixed = n_ref[...] - t_ref[...]
    for t in range(STEPS - 1):
        gradient = cnt_ref[t] * (NOISE_VAR * dual + fixed)
        velocity = MOMENTUM * velocity - STEP_SIZE * gradient
        dual = dual + velocity
        known_ref[t * 8 : (t + 1) * 8, :] = dual.astype(BF16)


def known_parts(index, targets, noise, dual, velocity):
    shape = dual.shape
    return pl.pallas_call(
        known_kernel,
        out_shape=(
            jax.ShapeDtypeStruct((STEPS,) + shape, F32),
            jax.ShapeDtypeStruct(((STEPS - 1) * shape[0], shape[1]), BF16),
        ),
        compiler_params=pltpu.CompilerParams(vmem_limit_bytes=32 << 20),
        cost_estimate=pl.CostEstimate(flops=1 << 23, bytes_accessed=1 << 20, transcendentals=0),
        name="known_parts",
    )(index, targets[None, :], noise, dual, velocity)


def place_kernel(i_ref, c_ref, *refs):
    o_ref = refs[-1]
    train = o_ref.shape[1]
    rows = jnp.concatenate([dot(c_ref[...], r_ref[...], NT) for r_ref in refs[:-1]], axis=1)
    tiles = spread(i_ref[...], rows, train)
    for h in range(train // 128):
        o_ref[:, h * 128 : (h + 1) * 128] = tiles[h * 8 : (h + 1) * 8, :]


def place(index, chooser, pieces, train):
    return pl.pallas_call(
        place_kernel,
        out_shape=jax.ShapeDtypeStruct((8, train), F32),
        compiler_params=pltpu.CompilerParams(vmem_limit_bytes=32 << 20),
        cost_estimate=pl.CostEstimate(flops=1 << 22, bytes_accessed=1 << 20, transcendentals=0),
        name="place",
    )(index[None, :], chooser, *pieces)


def finish_kernel(i_ref, r_ref, z0_ref, z1_ref, cnt_ref, t_ref, n_ref, a_ref, v_ref, ao_ref, vo_ref, rows_ref):
    train = a_ref.shape[1]
    for r in range(r_ref.shape[0]):
        block = jnp.sum(r_ref[r].astype(F32), axis=0)
        rows_ref[:4, r * 64 : (r + 1) * 64] = block[:, :64]
        rows_ref[4:, r * 64 : (r + 1) * 64] = block[:, 64:]
    rows = rows_ref[...]
    coarse = rows.astype(BF16).astype(F32)
    tiles = spread(i_ref[...], coarse, train) + spread(i_ref[...], rows - coarse, train)
    dual, velocity = a_ref[...], v_ref[...]
    fixed = n_ref[...] - t_ref[...]
    z0 = z0_ref[...]
    velocity = MOMENTUM * velocity - STEP_SIZE * (z0 + cnt_ref[0] * (NOISE_VAR * dual + fixed))
    dual = dual + velocity
    change = -STEP_SIZE * z0
    gradient = z1_ref[...] + cnt_ref[1] * (NOISE_VAR * (dual - change) + fixed)
    velocity = MOMENTUM * velocity - STEP_SIZE * gradient
    dual = dual + velocity
    base = cnt_ref[2] * (NOISE_VAR * dual + fixed)
    for h in range(train // 128):
        at = slice(h * 128, (h + 1) * 128)
        vo_ref[:, at] = MOMENTUM * velocity[:, at] - STEP_SIZE * (
            base[:, at] + tiles[h * 8 : (h + 1) * 8, :]
        )
    ao_ref[...] = dual + vo_ref[...]


def finish(index, rows, z0, z1, counts, targets, noise, dual, velocity):
    shape = jax.ShapeDtypeStruct(dual.shape, F32)
    return pl.pallas_call(
        finish_kernel,
        out_shape=(shape, shape),
        scratch_shapes=[pltpu.VMEM((8, rows.shape[0] * 64), F32)],
        compiler_params=pltpu.CompilerParams(vmem_limit_bytes=48 << 20),
        cost_estimate=pl.CostEstimate(flops=1 << 22, bytes_accessed=1 << 20, transcendentals=0),
        name="finish",
    )(index[None, :], rows, z0, z1, counts, targets[None, :], noise, dual, velocity)


def row_moves(dx, dz, dcore):
    return [
        ((x * 4 + z) * 2 + core, ((x + dx) % 4 * 4 + (z + dz) % 4) * 2 + (core ^ dcore))
        for x in range(4)
        for z in range(4)
        for core in range(2)
    ]


def from_x(block):
    return [block] + [lax.ppermute(block, "row", row_moves(d, 0, 0)) for d in (1, 2, 3)]


def from_z(block):
    return [block] + [lax.ppermute(block, "row", row_moves(0, d, 0)) for d in (1, 2, 3)]


def with_other_core(blocks):
    return blocks + [lax.ppermute(block, "row", row_moves(0, 0, 1)) for block in blocks]


def back_from(array, here, axis):
    turned = jnp.flip(array, axis)
    return lax.dynamic_slice_in_dim(jnp.concatenate([turned, turned], axis), 3 - here, 4, axis)


def after(*values):
    return lax.optimization_barrier(values)


def shards(
    x_train,
    targets,
    noise_draws,
    alpha_init,
    velocity_init,
    frequencies,
    phases,
    path_weights,
    x_window,
    batch_index,
):
    rows, cols = lax.axis_size("row"), lax.axis_size("col")
    row_id, col_id = lax.axis_index("row"), lax.axis_index("col")
    train = x_train.shape[1]
    batch_rows = batch_index.shape[1] // rows
    own_rows = batch_rows // cols
    group_rows = rows * own_rows
    paths = path_weights.shape[1]
    own_paths = paths // rows
    factor = (2.0 / (frequencies.shape[1] * cols)) ** 0.5
    dual, velocity, noise = alpha_init.T, velocity_init.T, noise_draws.T
    x_id, z_id, core_id = row_id // 8, row_id // 2 % 4, row_id % 2

    by_group = batch_index.reshape(STEPS, rows, cols, own_rows)
    mine = lax.dynamic_slice_in_dim(by_group, col_id, 1, 2)[:, :, 0] - col_id * train
    by_place = mine.reshape(STEPS, 4, 4, 2, own_rows)
    near = lax.dynamic_slice(by_place[0], (x_id, 0, core_id, 0), (1, 4, 1, own_rows)).reshape(-1)
    own_index = lax.dynamic_slice_in_dim(mine[1:], row_id, 1, 1).reshape(-1)
    own_index = jnp.concatenate([near, own_index])

    own_points, x_wide, f_wide = setup(own_index, x_train, frequencies, phases, cols)
    own_points, x_wide, dual, velocity, noise, mine = after(
        own_points, x_wide, dual, velocity, noise, mine
    )
    points = lax.all_to_all(own_points, "col", 0, 0, tiled=True)
    gathered0 = from_x(dual.astype(BF16))

    group_index = mine.reshape(STEPS, group_rows)
    counts, known = known_parts(group_index, targets, noise, dual, velocity)
    gathered = lax.all_gather(known, "row", axis=0, tiled=True).reshape(rows, STEPS - 1, own_paths, train)
    gathered1, gathered2 = (gathered[:, t].reshape(paths, train) for t in range(STEPS - 1))
    sorted_index = back_from(by_place[:2], x_id, 1)
    sorted_index = jnp.stack([sorted_index[0], back_from(sorted_index[1], z_id, 1)])
    sorted_index = sorted_index.transpose(0, 3, 1, 2, 4)
    sorted_index = jnp.where(core_id == 0, sorted_index, jnp.flip(sorted_index, 1)).reshape(2, group_rows)

    lane = lax.broadcasted_iota(jnp.int32, (128, 4), 0)
    back = lax.broadcasted_iota(jnp.int32, (128, 4), 1)
    path_of = ((x_id - lane // own_paths % 4) % 4 * 4 + (z_id - back) % 4) * 2 + (core_id ^ (lane // 32 % 2))
    path_of = path_of * own_paths + lane % own_paths
    here = lax.broadcasted_iota(jnp.int32, (paths // 4, paths), 1) == path_of[: paths // 4, :1]
    here = here.astype(BF16)
    window_part = window_prior(f_wide.T, path_weights, x_window, factor)
    points, window_part, path_of, here, sorted_index = after(points, window_part, path_of, here, sorted_index)
    prior_window = lax.psum_scatter(window_part, "col", scatter_dimension=0, tiled=True)
    gathered0 = jnp.concatenate(with_other_core(gathered0), axis=0)

    blocks = first_block(points, x_wide, gathered0, f_wide, path_weights, here, factor)
    row_index = lax.dynamic_slice_in_dim(batch_index[1], row_id * batch_rows, batch_rows, 0) - col_id * train

    def add_up(blocks):
        return jnp.sum(blocks.astype(F32), axis=0)

    chooser = lax.broadcasted_iota(jnp.int32, (own_paths, paths), 1)
    chooser = chooser - own_paths * row_id == lax.broadcasted_iota(jnp.int32, (own_paths, paths), 0)
    chooser = chooser.astype(BF16)

    blocks = lax.all_to_all(blocks, "col", 0, 0, tiled=True)
    group_points = pick_cols(sorted_index, x_train)
    blocks, group_points = after(blocks, group_points)
    terms0 = from_z(add_up(blocks).astype(BF16))
    between10 = pair_block(points, 4, group_points, 0, row_index[:, None], sorted_index[:1])
    *terms0, between10 = after(*terms0, between10)
    terms0 = from_x(merge(path_of, terms0))
    part1 = part_block(points, 4, x_wide, gathered1, f_wide, path_weights, factor)
    *terms0, part1 = after(*terms0, part1)
    terms0 = with_other_core(terms0)

    blocks = chain(part1, between10, terms0).reshape(cols, own_rows, paths)
    blocks = lax.all_to_all(blocks, "col", 0, 0, tiled=True)
    between21 = pair_block(points, 5, group_points, 1)
    blocks, between21 = after(blocks, between21)
    terms1 = from_z(add_up(blocks).astype(BF16))
    part2 = part_block(points, 5, x_wide, gathered2, f_wide, path_weights, factor)
    *terms1, part2 = after(*terms1, part2)
    terms1 = from_x(jnp.concatenate(terms1, axis=0))
    part2 = fold(part2, points, 5, group_points, 0, terms0)
    *terms1, part2 = after(*terms1, part2)
    terms1 = with_other_core(terms1)

    blocks = last(part2, between21, terms1).reshape(rows * cols, own_paths // 2, 2 * own_rows)
    blocks = lax.all_to_all(blocks, ("row", "col"), 0, 0, tiled=True)
    z0 = place(sorted_index[0], chooser, terms0, train)
    z1 = place(sorted_index[1], chooser, terms1, train)
    blocks, z0, z1 = after(blocks, z0, z1)
    blocks = blocks.reshape(rows, cols, own_paths // 2, 2 * own_rows)
    dual, velocity = finish(
        group_index[2], blocks, z0, z1, counts, targets, noise, dual, velocity
    )
    return (dual.T, velocity.T, prior_window)


def solution(mesh):
    placed = (
        P(None, "col"),
        P("col"),
        P("col", "row"),
        P("col", "row"),
        P("col", "row"),
        P(None, "col"),
        P("col"),
        P("col", None),
        P(None, "row"),
        P(),
    )
    return jax.shard_map(
        shards,
        mesh=mesh,
        in_specs=placed,
        out_specs=(P("col", "row"), P("col", "row"), P("col", "row")),
        check_vma=False,
    )
```
